32 devices in a mesh: groups: 2 (over y), az: 4 (over z), rg: 2 (over x), dates: 2 (over core).
Axes of the slice: x: 2, y: 2, z: 4, core: 2. Of those that a mesh axis runs over, the one named last changes fastest.
Arguments:
- phasor_sweep_volume: bfloat16 [128, 8, 24, 2, 512], P(('groups', 'az'), None, 'dates', None, 'rg'), parts along dimension 0, may hold values from -4 to 4
- sweep_patch_band: int32 [128, 1], P(('groups', 'az')), parts along dimension 0, may hold values from 0 to 3; in each aligned block of 16 rows (0 to 15, 16 to 31, ...) at most 8 rows name the same one
- sweep_strip_position: int32 [128], P(('groups', 'az')), parts along dimension 0, may hold values from 0 to 3
- master_slave_epochs: int32 [48, 2], P('dates'), may hold values from 0 to 23, all different within a row
Outputs:
- ml_coherence: float32 [48, 64, 32], P('dates', ('groups', 'az'), 'rg'), parts along dimension 1
- ml_interferogram: float32 [48, 2, 64, 32], P('dates', None, ('groups', 'az'), 'rg'), parts along dimension 2
The draws below stay inside these ranges and needn't reach their ends.
There are 2 independent parts, one for each index of `groups`. The reference program is written for one: setup_inputs(seed, part) draws one part's arguments, and reference() takes and returns one part's arrays. A program takes and returns all parts, laid end to end along the dimension named above; an argument that names none is the same for every part. Nothing has to cross between parts.
Inputs may be any that keep to these rules, and one draw needn't show every extreme that they name: `sweep_patch_band`: among the 16 bursts of one index of az, at most 8 name the same tile row, and some tile row is named by exactly 8 of them; every tile row is named by some burst. `master_slave_epochs`: the two dates of a pair differ; every date is in some pair.
All inputs are finite; a program needn't handle non-finite values.
Results may differ from the reference program's by a relative error of at most 0.0015.
Values may be sent and summed in bfloat16 or wider, within the bound.
No kernel may reach another device: no remote copies, remote signals or barrier semaphores. Data moves between devices by JAX's collectives and lax.ppermute only.
A program may use at most 64 MiB of HBM per device.

```python
import math
import jax
import jax.numpy as jnp
import numpy as np
from jax import lax

EPOCH_COUNT = 24
PAIRS = 48
SWEEP_HEIGHT = 8
STRIPS_IN_PATCH = 4
SWEEPS_IN_PIECE = 16
SA = 4
SR = 16
DISPATCH_CAP = 8
SWEEP_OVERALL = 64
NA = 128
SLANT_WIDTH = 512
N_AZ = 4


def draw_phasor_sweep_volume(key, part):
    key = jax.random.fold_in(key, 7)
    acquisition_seed, key_noise, key_level = jax.random.split(key, 3)
    tensor_extent = (SWEEP_OVERALL, SWEEP_HEIGHT, EPOCH_COUNT, 2, SLANT_WIDTH)
    level = jnp.exp(jax.random.uniform(key_level, (1, 1, EPOCH_COUNT, 1, 1), jnp.float32, math.log(0.3), math.log(1.5)))
    acquisition_volume = jax.random.normal(acquisition_seed, (SWEEP_OVERALL, SWEEP_HEIGHT, 1, 2, SLANT_WIDTH), jnp.float32)
    noise = jax.random.normal(key_noise, tensor_extent, jnp.float32)
    values = 0.5 * (acquisition_volume + level * noise)
    return jnp.clip(values, -4.0, 4.0).astype(jnp.bfloat16)


def place_ends(array, key, least, largest):
    index_at = [jax.random.randint(jax.random.fold_in(key, axis), (), 0, length) for axis, length in enumerate(array.shape)]
    longest = array.shape.index(max(array.shape))
    neighbour = index_at[:longest] + [(index_at[longest] + 1) % array.shape[longest]] + index_at[longest + 1:]
    return array.at[tuple(index_at)].set(least).at[tuple(neighbour)].set(largest)


def different_ones(stream_key, rows, count, top, lift):
    ranking = jax.random.permutation(jax.random.fold_in(stream_key, 1), count)
    favour = ranking
    for power in range(3):
        favour = favour * favour // count
    favour = favour * lift // count
    chance = jax.random.randint(jax.random.fold_in(stream_key, 2), (rows, count), 0, 4096) + favour
    fixed_rows = jax.random.permutation(jax.random.fold_in(stream_key, 3), rows)[jnp.arange(count) % rows]
    chance = jnp.where(jnp.arange(rows)[:, None] == fixed_rows[None, :], 1 << 14, chance)
    priority = chance * count + jnp.arange(count)
    return lax.top_k(priority.astype(jnp.int32), top)[1].astype(jnp.int32)


def deal_out(key, own, number, rows, amount, top, reach, skew):
    sequence = jax.random.permutation(key, amount)
    packed, ordinary = shares(amount, rows * top, reach, skew, True), shares(amount, rows * top, reach, skew, False)
    places = jnp.arange(amount)

    def named(lengths, turn):
        used = int((lengths > 0).sum())
        fixed = max(1, used // 4)
        shifted = fixed + (places - fixed + turn * (used - fixed)) % max(1, amount - fixed)
        return jnp.zeros((amount,), jnp.int32).at[sequence[jnp.where(places < fixed, places, shifted)]].set(jnp.asarray(lengths, jnp.int32))

    lengths = jnp.where(number % 4 == 0, named(packed, number // 4), named(ordinary, number - number // 4 - 1))
    mixed = jax.random.permutation(jax.random.fold_in(own, 3), amount)
    donor, sink = mixed[0:amount // 2 * 2:2], mixed[1:amount // 2 * 2:2]
    slack = jnp.minimum(lengths[donor] - 1, reach - lengths[sink]) // 2
    slack = jnp.where((donor == sequence[0]) | (sink == sequence[0]) | (lengths[sink] == 0), 0, jnp.maximum(slack, 0))
    shifted = jax.random.randint(jax.random.fold_in(own, 4), (amount // 2,), 0, 1 << 20) % (slack + 1)
    lengths = lengths.at[donor].add(-shifted).at[sink].add(shifted)
    items = jnp.searchsorted(jnp.cumsum(lengths), jnp.arange(rows * top), side="right").astype(jnp.int32)
    table = items.reshape(top, rows).T
    table = table[jax.random.permutation(jax.random.fold_in(own, 1), rows)]
    turn = jax.random.randint(jax.random.fold_in(own, 2), (rows, 1), 0, top)
    return jnp.take_along_axis(table, (jnp.arange(top)[None, :] + turn) % top, axis=1)


def shares(count, total, reach, lean, full):
    weights = [(1 << 20) // math.isqrt(rank ** lean) + 1 for rank in range(1, count + 1)]
    largest = reach if full else min(reach, max(-(-total // count), total * weights[0] // sum(weights)))
    least = 1 if total - largest >= count - 1 else 0
    given, rest = [largest] + [least] * (count - 1), total - largest - least * (count - 1)
    while rest > 0:
        movable = [i for i in range(1, count) if given[i] < largest] or [i for i in range(1, count) if given[i] < reach]
        pool, left = sum([weights[i] for i in movable]), rest
        for i in movable:
            more = min(reach - given[i], max(1, left * weights[i] // pool), rest)
            given[i] = given[i] + more
            rest = rest - more
    return np.array(given)


def setup_inputs(seed: int = 0, part: int = 0) -> dict:
    seeds = jax.random.split(jax.random.key(seed), 5)
    part_splits = jax.random.split(jax.random.fold_in(seeds[4], part), 5)
    phasor_sweep_volume = draw_phasor_sweep_volume(jax.random.fold_in(jax.random.fold_in(seeds[4], part), 71), part)
    sweep_patch_band_keys = jax.random.split(jax.random.fold_in(part_splits[1], 1), SWEEP_OVERALL // SWEEPS_IN_PIECE)
    sweep_patch_band_turns = jax.random.permutation(jax.random.fold_in(part_splits[1], 3), SWEEP_OVERALL // SWEEPS_IN_PIECE)
    sweep_patch_band = jax.vmap(lambda own, number: deal_out(jax.random.fold_in(part_splits[1], 2), own, number, SWEEPS_IN_PIECE, N_AZ, 1, DISPATCH_CAP, 2))(sweep_patch_band_keys, sweep_patch_band_turns).reshape((SWEEP_OVERALL, 1))
    sweep_strip_position = place_ends(jax.random.randint(part_splits[2], (SWEEP_OVERALL,), 0, STRIPS_IN_PATCH), jax.random.fold_in(part_splits[2], 1), 0, STRIPS_IN_PATCH - 1).astype(jnp.int32)
    master_slave_epochs = different_ones(seeds[3], PAIRS, EPOCH_COUNT, 2, 0)
    return dict(phasor_sweep_volume=phasor_sweep_volume, sweep_patch_band=sweep_patch_band, sweep_strip_position=sweep_strip_position, master_slave_epochs=master_slave_epochs)


def reference(phasor_sweep_volume, sweep_patch_band, sweep_strip_position, master_slave_epochs):
    strip_segment = (sweep_patch_band[:, 0] * STRIPS_IN_PATCH + sweep_strip_position).astype(jnp.int32)
    boxcar_accumulated = jax.ops.segment_sum(phasor_sweep_volume.astype(jnp.float32), strip_segment, num_segments=N_AZ * STRIPS_IN_PATCH)
    stitched = boxcar_accumulated.reshape(NA, EPOCH_COUNT, 2, SLANT_WIDTH).astype(jnp.bfloat16)

    def one_pair(pair):
        first = lax.dynamic_index_in_dim(stitched, pair[0], 1, keepdims=False).astype(jnp.float32)
        second = lax.dynamic_index_in_dim(stitched, pair[1], 1, keepdims=False).astype(jnp.float32)
        first_re, first_im = (first[:, 0], first[:, 1])
        second_re, second_im = (second[:, 0], second[:, 1])
        real_part = first_re * second_re + first_im * second_im
        imag_part = first_im * second_re - first_re * second_im
        power_a = first_re * first_re + first_im * first_im
        power_b = second_re * second_re + second_im * second_im
        stacked = jnp.stack([real_part, imag_part, power_a, power_b])
        padded = jnp.pad(stacked, ((0, 0), (2, 2), (10, 10)))
        along = padded[:, 0:NA, :]
        for shift in range(1, 5):
            along = along + padded[:, shift:shift + NA, :]
        boxed = along[:, :, 0:SLANT_WIDTH]
        for shift in range(1, 21):
            boxed = boxed + along[:, :, shift:shift + SLANT_WIDTH]
        boxed = boxed / 105.0
        coherence = jnp.sqrt(boxed[0] * boxed[0] + boxed[1] * boxed[1]) / jnp.sqrt(boxed[2] * boxed[3] + 1e-06)
        looked = coherence.reshape(NA // SA, SA, SLANT_WIDTH // SR, SR).mean(axis=(1, 3))
        product_looks = stacked[0:2].reshape(2, NA // SA, SA, SLANT_WIDTH // SR, SR).mean(axis=(2, 4))
        return (looked, product_looks)
    ml_coherence, ml_interferogram = lax.map(one_pair, master_slave_epochs)
    return (ml_coherence, ml_interferogram)
```

```python
import functools

import jax
import jax.numpy as jnp
from jax import lax
from jax.experimental import pallas as pl
from jax.experimental.pallas import tpu as pltpu
from jax.sharding import PartitionSpec as P

STRIPS = 4
SA = 4
SR = 16
HA = 2
HR = 10
LANES = 128
F32 = jnp.float32
BF16 = jnp.bfloat16
CHUNKS = ((0, 3), (1, 2))
ROLE_ROWS = ((0, 2, 3, 1), (1, 0, 2, 3), (3, 2, 0, 1), (1, 3, 2, 0))
ROLE_BITS = sum(role << (2 * (4 * i + j)) for i, row in enumerate(ROLE_ROWS) for j, role in enumerate(row))
ROLE_BITS = ROLE_BITS - (1 << 32) if ROLE_BITS >= 1 << 31 else ROLE_BITS


def params():
    return pltpu.CompilerParams(vmem_limit_bytes=56 * 1024 * 1024)


def vmem():
    return pl.BlockSpec(memory_space=pltpu.VMEM)


def smem():
    return pl.BlockSpec(memory_space=pltpu.SMEM)


def partial_kernel(line, count, me_ref, band_ref, strip_ref, x_ref, *refs):
    outs, total = refs[:-1], refs[-1]
    total[...] = jnp.zeros_like(total)

    def add(b, carry):
        target = band_ref[b]
        if line:
            shift = 2 * (4 * me_ref[0] + target)
            target = lax.shift_right_logical(jnp.int32(ROLE_BITS), shift) & 3
        slot = target * STRIPS + strip_ref[b]
        total[slot] += x_ref[b].astype(F32)
        return carry

    lax.fori_loop(0, x_ref.shape[0], add, 0)
    for role in range(count):
        for c, strips in enumerate(CHUNKS):
            for s, strip in enumerate(strips):
                value = total[role * STRIPS + strip].astype(BF16)
                if line:
                    outs[role * len(CHUNKS) + c][s] = value
                else:
                    outs[c][role, s] = value


def partial_sums(line, count, me, band, strip, x):
    rows = x.shape[1]
    if line:
        shapes = [(2, rows, LANES)] * (count * len(CHUNKS))
    else:
        shapes = [(count, 2, rows, LANES)] * len(CHUNKS)
    return pl.pallas_call(
        functools.partial(partial_kernel, line, count),
        out_shape=[jax.ShapeDtypeStruct(s, BF16) for s in shapes],
        in_specs=[smem(), smem(), smem(), vmem()],
        out_specs=[vmem()] * len(shapes),
        scratch_shapes=[pltpu.VMEM((count * STRIPS, rows, LANES), F32)],
        compiler_params=params(),
        name="partial_sums",
    )(me, band, strip, x)


def line_exchange(parts, me):
    own, first, side, far = parts
    ends = (me == 0) | (me == 3)
    near = lax.ppermute(first, "az", [(0, 1), (1, 0), (2, 3), (3, 2)])
    middle = lax.ppermute(side, "az", [(1, 2), (2, 1)])
    joined = jnp.where(ends, far, (far.astype(F32) + near.astype(F32)).astype(BF16))
    across = lax.ppermute(joined, "az", [(0, 2), (2, 0), (1, 3), (3, 1)])
    outer = lax.ppermute(side, "az", [(0, 1), (3, 2)])
    total = own.astype(F32) + across.astype(F32)
    total = total + jnp.where(ends, near.astype(F32), middle.astype(F32) + outer.astype(F32))
    return total.astype(BF16)


def plain_exchange(parts):
    arrived = lax.all_to_all(parts, "az", split_axis=0, concat_axis=0, tiled=True)
    return jnp.sum(arrived.astype(F32), axis=0).astype(BF16)


def pack_kernel(lines, outer, inner, top, bottom, *refs):
    places, packed = refs[: len(refs) // 2], refs[len(refs) // 2 :]
    rows = top.shape[0] // HA
    height = outer.shape[1] // rows

    def line(at):
        if at < 0:
            return top[(at + HA) * rows : (at + HA + 1) * rows]
        if at >= lines:
            return bottom[(at - lines) * rows : (at - lines + 1) * rows]
        strip, within = divmod(at, height)
        ref, where = {0: (outer, 0), 3: (outer, 1), 1: (inner, 0), 2: (inner, 1)}[strip]
        return ref[where, within * rows : (within + 1) * rows]

    for place, out in zip(places, packed):
        for group in range(STRIPS):
            spread = jnp.concatenate(
                [line(height * group - HA + i) for i in range(height + 2 * HA)], axis=1
            )
            out[group] = jnp.dot(spread, place[...], preferred_element_type=F32).astype(BF16)


def pack_edges(lines, outer, inner, top, bottom, places):
    rows = top.shape[0] // HA
    return pl.pallas_call(
        functools.partial(pack_kernel, lines),
        out_shape=[jax.ShapeDtypeStruct((STRIPS, rows, LANES), BF16)] * len(places),
        in_specs=[vmem()] * (4 + len(places)),
        out_specs=[vmem()] * len(places),
        compiler_params=params(),
        name="pack_edges",
    )(outer, inner, top, bottom, *places)


def box_kernel(sides, lines, core_ref, side_ref, epochs, *refs):
    (outer, outer2, inner, inner2, top, top2, bottom, bottom2), refs = refs[:8], refs[8:]
    halos, refs = refs[: 2 * sides], refs[2 * sides :]
    coherence_ref, product_ref, stack, prod, left, edge, coh, looked = refs
    rows = top.shape[0] // HA
    both = 2 * rows
    pairs = epochs.shape[0]
    dates = both // 4
    height = lines // STRIPS
    span = height + 2 * HA
    cols = 2 * LANES
    looks = lines // SA

    for half, (e, m, t, b) in enumerate(
        ((outer, inner, top, bottom), (outer2, inner2, top2, bottom2))
    ):
        at = half * rows
        for i in range(HA):
            stack[i, at : at + rows] = t[i * rows : (i + 1) * rows]
            stack[HA + lines + i, at : at + rows] = b[i * rows : (i + 1) * rows]
        for strip in range(STRIPS):
            ref, where = {0: (e, 0), 3: (e, 1), 1: (m, 0), 2: (m, 1)}[strip]
            for i in range(height):
                stack[HA + strip * height + i, at : at + rows] = ref[
                    where, i * rows : (i + 1) * rows
                ]

    turned = epochs[...] - (dates // 2) * core_ref[0]
    turned = jnp.where(turned < 0, turned + dates, turned) * 4
    first, second = turned[:, 0:1], turned[:, 1:2]

    def picker(offsets):
        wanted = jnp.concatenate([d + o for d in (first, second) for o in offsets], axis=0)
        column = lax.broadcasted_iota(jnp.int32, (wanted.shape[0], both), 1)
        return jnp.where(column == wanted, 1.0, 0.0).astype(BF16)

    def fields(ar, ai, br, bi):
        return ar * br + ai * bi, ai * br - ar * bi, ar * ar + ai * ai, br * br + bi * bi

    pick = picker((0, 1, 2, 3))

    def products(i, carry):
        two = jnp.concatenate([stack[2 * i], stack[2 * i + 1]], axis=1)
        got = jnp.dot(pick, two, preferred_element_type=F32)
        part = [got[q * pairs : (q + 1) * pairs] for q in range(8)]
        for ct in range(2):
            parts = fields(part[2 * ct], part[2 * ct + 1], part[4 + 2 * ct], part[5 + 2 * ct])
            for f, value in enumerate(parts):
                at = slice(f * pairs, (f + 1) * pairs)
                lane = slice(ct * LANES, (ct + 1) * LANES)
                prod[2 * i, at, lane] = value[:, :LANES]
                prod[2 * i + 1, at, lane] = value[:, LANES:]
        return carry

    lax.fori_loop(0, (lines + 2 * HA) // 2, products, 0, unroll=2)

    def split(value):
        high = value.astype(BF16)
        return high, (value - high.astype(F32)).astype(BF16)

    for s in range(sides):
        base = side_ref[s] * 2
        chosen = picker((base, base + 1))
        for group in range(STRIPS):
            packed = jnp.concatenate([halos[2 * s][group], halos[2 * s + 1][group]], axis=0)
            got = jnp.dot(chosen, packed, preferred_element_type=F32)
            part = [got[q * pairs : (q + 1) * pairs] for q in range(4)]
            high, low = split(jnp.concatenate(fields(*part), axis=0))
            edge[s, group, :, :LANES] = high
            edge[s, group, :, LANES:] = low

    def azimuth(g, carry):
        for c in range(4 * pairs // 16):
            at = slice(16 * c, 16 * c + 16)
            p = [prod[SA * g + i, at, :] for i in range(SA + 2 * HA)]
            a01, a23, a45, a67 = p[0] + p[1], p[2] + p[3], p[4] + p[5], p[6] + p[7]
            out = (a01 + a23 + p[4], p[1] + a23 + a45, a23 + a45 + p[6], p[3] + a45 + a67)
            for j in range(SA):
                high, low = split(out[j])
                left[lax.rem(g, 2) * SA + j, lax.div(g, 2), at, :cols] = high
                left[lax.rem(g, 2) * SA + j, lax.div(g, 2), at, cols:] = low
            if c < 2 * pairs // 16:
                looked[g, at, :] = a23 + a45
        return carry

    lax.fori_loop(0, looks, azimuth, 0)

    row = lax.broadcasted_iota(jnp.int32, (cols, cols), 0)
    col = lax.broadcasted_iota(jnp.int32, (cols, cols), 1)

    def ones(condition):
        return jnp.where(condition, 1.0, 0.0).astype(BF16)

    band = ones(jnp.abs(row - col) <= HR)
    lane = row & (LANES - 1)
    line_at = lax.div(lane, HR)
    column_at = lane - line_at * HR
    inside = lane < span * HR
    reach = []
    for s in range(sides):
        low_side = inside & (col <= column_at)
        high_side = inside & (col - (cols - HR) >= column_at)
        reach.append(
            jnp.where(side_ref[s] == 0, jnp.where(high_side, 1, 0), jnp.where(low_side, 1, 0))
        )

    scale = 1.0 / float((2 * HA + 1) * (2 * HR + 1)) ** 2
    for k in range(height):
        boxed = jnp.dot(
            left[k].reshape(STRIPS * 4 * pairs, 2 * cols),
            jnp.concatenate([band, band], axis=0),
            preferred_element_type=F32,
        )
        for s in range(sides):
            near = ones((reach[s] == 1) & (line_at >= k) & (line_at <= k + 2 * HA))
            boxed = boxed + jnp.dot(
                edge[s].reshape(STRIPS * 4 * pairs, cols), near, preferred_element_type=F32
            )
        for group in range(STRIPS):
            at = group * 4 * pairs
            re, im, pa, pb = [
                boxed[at + f * pairs : at + (f + 1) * pairs] for f in range(4)
            ]
            value = jnp.sqrt((re * re + im * im) * scale) * lax.rsqrt(pa * pb * scale + 1e-6)
            look = (height // SA) * group + k // SA
            if k % SA == 0:
                coh[look] = value
            else:
                coh[look] += value

    gather = ones(
        lax.div(lax.broadcasted_iota(jnp.int32, (cols, cols // SR), 0), SR)
        == lax.broadcasted_iota(jnp.int32, (cols, cols // SR), 1)
    )

    def mean(value):
        high, low = split(value)
        out = jnp.dot(high, gather, preferred_element_type=F32)
        out = out + jnp.dot(low, gather, preferred_element_type=F32)
        return out * (1.0 / (SA * SR))

    coh_mean = mean(coh[...].reshape(looks * pairs, cols))
    product_mean = mean(looked[...].reshape(looks * 2 * pairs, cols))
    for g in range(looks):
        coherence_ref[:, g, :] = coh_mean[g * pairs : (g + 1) * pairs]
        product_ref[:, 0, g, :] = product_mean[2 * g * pairs : (2 * g + 1) * pairs]
        product_ref[:, 1, g, :] = product_mean[(2 * g + 1) * pairs : (2 * g + 2) * pairs]


def boxes(lines, core, side, epochs, tiles, halos):
    pairs = epochs.shape[0]
    sides = len(halos) // 2
    rows = tiles[4].shape[0] // HA
    cols = 2 * LANES
    looks = lines // SA
    height = lines // STRIPS
    return pl.pallas_call(
        functools.partial(box_kernel, sides, lines),
        out_shape=[
            jax.ShapeDtypeStruct((pairs, looks, cols // SR), F32),
            jax.ShapeDtypeStruct((pairs, 2, looks, cols // SR), F32),
        ],
        in_specs=[smem(), smem()] + [vmem()] * (1 + len(tiles) + len(halos)),
        out_specs=[vmem(), vmem()],
        scratch_shapes=[
            pltpu.VMEM((lines + 2 * HA, 2 * rows, LANES), BF16),
            pltpu.VMEM((lines + 2 * HA, 4 * pairs, cols), F32),
            pltpu.VMEM((height, STRIPS, 4 * pairs, 2 * cols), BF16),
            pltpu.VMEM((sides, STRIPS, 4 * pairs, cols), BF16),
            pltpu.VMEM((looks, pairs, cols), F32),
            pltpu.VMEM((looks, 2 * pairs, cols), F32),
        ],
        compiler_params=params(),
        name="boxes",
    )(core, side, epochs, *tiles, *halos)


def edge_place(start):
    span = LANES // HR
    row = jnp.arange(span * LANES, dtype=jnp.int32)
    column = (row % LANES) - start
    target = jnp.where((column >= 0) & (column < HR), (row // LANES) * HR + column, -1)
    return (target[:, None] == jnp.arange(LANES, dtype=jnp.int32)[None, :]).astype(BF16)


def per_device(volume, band, strip, epochs):
    bursts, height, dates, _, columns = volume.shape
    count, wide = lax.axis_size("az"), lax.axis_size("rg")
    assert columns == 2 * LANES
    lines = STRIPS * height
    rows = dates * 4
    me, rg, core = lax.axis_index("az"), lax.axis_index("rg"), lax.axis_index("dates")
    x = volume.reshape(bursts, height, dates, 2, 2, LANES).transpose(0, 1, 2, 4, 3, 5)
    x = x.reshape(bursts, height * rows, LANES)
    line = count == 4
    parts = partial_sums(line, count, me.reshape(1), band.reshape(-1), strip, x)
    if line:
        outer = line_exchange(parts[0::2], me)
        inner = line_exchange(parts[1::2], me)
    else:
        outer, inner = [plain_exchange(p) for p in parts]
    step = [(i, i + 1) for i in range(count - 1)]
    top = lax.ppermute(outer[1, (height - HA) * rows :], "az", step)
    bottom = lax.ppermute(outer[0, : HA * rows], "az", [(j, i) for i, j in step])
    swap = [(0, 1), (1, 0)]
    other = lambda v: lax.ppermute(v, "dates", swap)
    if wide == 2:
        side = rg.reshape(1)
        places = [edge_place(jnp.where(rg == 0, LANES - HR, 0))]
        moves = [[(0, 1), (1, 0)]]
    else:
        side = jnp.arange(2, dtype=jnp.int32)
        places = [edge_place(0), edge_place(LANES - HR)]
        up = [(i, i + 1) for i in range(wide - 1)]
        moves = [[(j, i) for i, j in up], up]
    packed = pack_edges(lines, outer, inner, top, bottom, places)
    halos = []
    for value, move in zip(packed, moves):
        halos.append(lax.ppermute(value, "rg", move))
        both = [(2 * i + c, 2 * j + 1 - c) for i, j in move for c in range(2)]
        halos.append(lax.ppermute(value, ("rg", "dates"), both))
    tiles = [
        outer, other(outer), inner, other(inner), top, other(top), bottom, other(bottom),
    ]
    return tuple(boxes(lines, core.reshape(1), side, epochs, tiles, halos))


def solution(mesh):
    return jax.shard_map(
        per_device,
        mesh=mesh,
        in_specs=(
            P(("groups", "az"), None, "dates", None, "rg"),
            P(("groups", "az"), None),
            P(("groups", "az")),
            P("dates", None),
        ),
        out_specs=(P("dates", ("groups", "az"), "rg"), P("dates", None, ("groups", "az"), "rg")),
        check_vma=False,
    )
```

```python
import functools

import jax
import jax.numpy as jnp
from jax import lax
from jax.experimental import pallas as pl
from jax.experimental.pallas import tpu as pltpu
from jax.sharding import PartitionSpec as P

STRIPS = 4
SA = 4
SR = 16
HA = 2
HR = 10
LANES = 128
F32 = jnp.float32
BF16 = jnp.bfloat16
CHUNKS = ((0, 3), (1, 2))
ROLE_ROWS = ((0, 2, 3, 1), (1, 0, 2, 3), (3, 2, 0, 1), (1, 3, 2, 0))
ROLE_BITS = sum(role << (2 * (4 * i + j)) for i, row in enumerate(ROLE_ROWS) for j, role in enumerate(row))
ROLE_BITS = ROLE_BITS - (1 << 32) if ROLE_BITS >= 1 << 31 else ROLE_BITS


def params():
    return pltpu.CompilerParams(vmem_limit_bytes=28 * 1024 * 1024)


def vmem():
    return pl.BlockSpec(memory_space=pltpu.VMEM)


def in_vmem(value):
    return pltpu.with_memory_space_constraint(value, pltpu.VMEM)


def smem():
    return pl.BlockSpec(memory_space=pltpu.SMEM)


def partial_kernel(line, count, me_ref, band_ref, strip_ref, x_ref, *refs):
    outs, total = refs[:-1], refs[-1]
    total[...] = jnp.zeros_like(total)

    def add(b, carry):
        target = band_ref[b]
        if line:
            shift = 2 * (4 * me_ref[0] + target)
            target = lax.shift_right_logical(jnp.int32(ROLE_BITS), shift) & 3
        slot = target * STRIPS + strip_ref[b]
        total[slot] += x_ref[b].astype(F32)
        return carry

    lax.fori_loop(0, x_ref.shape[0], add, 0)
    for role in range(count):
        for c, strips in enumerate(CHUNKS):
            for s, strip in enumerate(strips):
                value = total[role * STRIPS + strip].astype(BF16)
                if line:
                    outs[role * len(CHUNKS) + c][s] = value
                else:
                    outs[c][role, s] = value


def partial_sums(line, count, me, band, strip, x):
    rows = x.shape[1]
    if line:
        shapes = [(2, rows, LANES)] * (count * len(CHUNKS))
    else:
        shapes = [(count, 2, rows, LANES)] * len(CHUNKS)
    return pl.pallas_call(
        functools.partial(partial_kernel, line, count),
        out_shape=[jax.ShapeDtypeStruct(s, BF16) for s in shapes],
        in_specs=[smem(), smem(), smem(), vmem()],
        out_specs=[vmem()] * len(shapes),
        scratch_shapes=[pltpu.VMEM((count * STRIPS, rows, LANES), F32)],
        compiler_params=params(),
        name="partial_sums",
    )(me, band, strip, x)


def joined_sum(ends, parts):
    own, near, middle, across, outer = [p.astype(F32) for p in parts]
    return (own + across + jnp.where(ends, near, middle + outer)).astype(BF16)


def line_exchange(parts, ends):
    own, first, side, far = [parts[2 * i : 2 * i + 2] for i in range(4)]
    near = [lax.ppermute(v, "az", [(0, 1), (1, 0), (2, 3), (3, 2)]) for v in first]
    middle = [lax.ppermute(v, "az", [(1, 2), (2, 1)]) for v in side]
    chunks, last = [], None
    for c in range(2):
        own_far = far[c]
        if last is not None:
            own_far, last = lax.optimization_barrier((own_far, last))
        joined = jnp.where(ends, own_far, (own_far.astype(F32) + near[c].astype(F32)).astype(BF16))
        joined, held = lax.optimization_barrier((joined, side[c]))
        last = joined
        across = lax.ppermute(joined, "az", [(0, 2), (2, 0), (1, 3), (3, 1)])
        outer = lax.ppermute(held, "az", [(0, 1), (3, 2)])
        chunks.append((own[c], near[c], middle[c], across, outer))
    return chunks


def plain_exchange(parts):
    arrived = lax.all_to_all(parts, "az", split_axis=0, concat_axis=0, tiled=True)
    return jnp.sum(arrived.astype(F32), axis=0).astype(BF16)


def finish_kernel(lines, line, ends_ref, outer, top, bottom, *refs):
    parts, refs = refs[: 5 if line else 1], refs[5 if line else 1 :]
    inner, packed = refs[len(refs) // 2], refs[len(refs) // 2 + 1 :]
    places = refs[: len(packed)]
    rows = top.shape[0] // HA
    height = outer.shape[1] // rows
    if line:
        own, near, middle, across, other = [p[...].astype(F32) for p in parts]
        total = own + across + jnp.where(ends_ref[0] == 1, near, middle + other)
    else:
        total = parts[0][0].astype(F32)
        for i in range(1, parts[0].shape[0]):
            total = total + parts[0][i].astype(F32)
    inner[...] = total.astype(BF16)

    def one(at):
        if at < 0:
            return top[(at + HA) * rows : (at + HA + 1) * rows]
        if at >= lines:
            return bottom[(at - lines) * rows : (at - lines + 1) * rows]
        strip, within = divmod(at, height)
        ref, where = {0: (outer, 0), 3: (outer, 1), 1: (inner, 0), 2: (inner, 1)}[strip]
        return ref[where, within * rows : (within + 1) * rows]

    spread = jnp.concatenate(
        [
            jnp.concatenate([one(height * g - HA + i) for i in range(height + 2 * HA)], axis=1)
            for g in range(STRIPS)
        ],
        axis=0,
    )
    for place, out in zip(places, packed):
        got = jnp.dot(spread, place[...], preferred_element_type=F32).astype(BF16)
        for g in range(STRIPS):
            out[g] = got[g * rows : (g + 1) * rows]


def finish(lines, line, ends, outer, top, bottom, parts, places):
    rows = top.shape[0] // HA
    tile = (STRIPS, rows, LANES)
    operands = [in_vmem(v) for v in (outer, top, bottom, *parts, *places)]
    return pl.pallas_call(
        functools.partial(finish_kernel, lines, line),
        out_shape=[pltpu.VMEM(outer.shape, BF16)] + [pltpu.VMEM(tile, BF16)] * len(places),
        in_specs=[smem()] + [vmem()] * len(operands),
        out_specs=[vmem()] * (1 + len(places)),
        compiler_params=params(),
        name="finish",
    )(ends, *operands)


def box_kernel(sides, lines, core_ref, side_ref, epochs, *refs):
    (outer, outer2, inner, inner2, top, top2, bottom, bottom2), refs = refs[:8], refs[8:]
    halos, refs = refs[: 2 * sides], refs[2 * sides :]
    coherence_ref, product_ref, stack, prod, left, edge, coh, looked = refs
    rows = top.shape[0] // HA
    both = 2 * rows
    pairs = epochs.shape[0]
    dates = both // 4
    height = lines // STRIPS
    span = height + 2 * HA
    cols = 2 * LANES
    looks = lines // SA

    for half, (e, m, t, b) in enumerate(
        ((outer, inner, top, bottom), (outer2, inner2, top2, bottom2))
    ):
        at = half * rows
        for i in range(HA):
            stack[i, at : at + rows] = t[i * rows : (i + 1) * rows]
            stack[HA + lines + i, at : at + rows] = b[i * rows : (i + 1) * rows]
        for strip in range(STRIPS):
            ref, where = {0: (e, 0), 3: (e, 1), 1: (m, 0), 2: (m, 1)}[strip]
            for i in range(height):
                stack[HA + strip * height + i, at : at + rows] = ref[
                    where, i * rows : (i + 1) * rows
                ]

    turned = epochs[...] - (dates // 2) * core_ref[0]
    turned = jnp.where(turned < 0, turned + dates, turned) * 4
    first, second = turned[:, 0:1], turned[:, 1:2]

    def picker(offsets):
        wanted = jnp.concatenate([d + o for d in (first, second) for o in offsets], axis=0)
        column = lax.broadcasted_iota(jnp.int32, (wanted.shape[0], both), 1)
        return jnp.where(column == wanted, 1.0, 0.0).astype(BF16)

    def fields(ar, ai, br, bi):
        return ar * br + ai * bi, ai * br - ar * bi, ar * ar + ai * ai, br * br + bi * bi

    pick = picker((0, 1, 2, 3))

    def products(i, carry):
        two = jnp.concatenate([stack[2 * i], stack[2 * i + 1]], axis=1)
        got = jnp.dot(pick, two, preferred_element_type=F32)
        part = [got[q * pairs : (q + 1) * pairs] for q in range(8)]
        for ct in range(2):
            parts = fields(part[2 * ct], part[2 * ct + 1], part[4 + 2 * ct], part[5 + 2 * ct])
            for f, value in enumerate(parts):
                at = slice(f * pairs, (f + 1) * pairs)
                lane = slice(ct * LANES, (ct + 1) * LANES)
                prod[2 * i, at, lane] = value[:, :LANES]
                prod[2 * i + 1, at, lane] = value[:, LANES:]
        return carry

    lax.fori_loop(0, (lines + 2 * HA) // 2, products, 0, unroll=2)

    def split(value):
        high = value.astype(BF16)
        return high, (value - high.astype(F32)).astype(BF16)

    for s in range(sides):
        base = side_ref[s] * 2
        chosen = picker((base, base + 1))
        for group in range(STRIPS):
            packed = jnp.concatenate([halos[2 * s][group], halos[2 * s + 1][group]], axis=0)
            got = jnp.dot(chosen, packed, preferred_element_type=F32)
            part = [got[q * pairs : (q + 1) * pairs] for q in range(4)]
            high, low = split(jnp.concatenate(fields(*part), axis=0))
            edge[s, group, :, :LANES] = high
            edge[s, group, :, LANES:] = low

    def azimuth(g, carry):
        for c in range(4 * pairs // 16):
            at = slice(16 * c, 16 * c + 16)
            p = [prod[SA * g + i, at, :] for i in range(SA + 2 * HA)]
            a01, a23, a45, a67 = p[0] + p[1], p[2] + p[3], p[4] + p[5], p[6] + p[7]
            out = (a01 + a23 + p[4], p[1] + a23 + a45, a23 + a45 + p[6], p[3] + a45 + a67)
            for j in range(SA):
                high, low = split(out[j])
                left[lax.rem(g, 2) * SA + j, lax.div(g, 2), at, :cols] = high
                left[lax.rem(g, 2) * SA + j, lax.div(g, 2), at, cols:] = low
            if c < 2 * pairs // 16:
                looked[g, at, :] = a23 + a45
        return carry

    lax.fori_loop(0, looks, azimuth, 0)

    row = lax.broadcasted_iota(jnp.int32, (cols, cols), 0)
    col = lax.broadcasted_iota(jnp.int32, (cols, cols), 1)

    def ones(condition):
        return jnp.where(condition, 1.0, 0.0).astype(BF16)

    band = ones(jnp.abs(row - col) <= HR)
    lane = row & (LANES - 1)
    line_at = lax.div(lane, HR)
    column_at = lane - line_at * HR
    inside = lane < span * HR
    reach = []
    for s in range(sides):
        low_side = inside & (col <= column_at)
        high_side = inside & (col - (cols - HR) >= column_at)
        reach.append(
            jnp.where(side_ref[s] == 0, jnp.where(high_side, 1, 0), jnp.where(low_side, 1, 0))
        )

    scale = 1.0 / float((2 * HA + 1) * (2 * HR + 1)) ** 2
    for k in range(height):
        boxed = jnp.dot(
            left[k].reshape(STRIPS * 4 * pairs, 2 * cols),
            jnp.concatenate([band, band], axis=0),
            preferred_element_type=F32,
        )
        for s in range(sides):
            near = ones((reach[s] == 1) & (line_at >= k) & (line_at <= k + 2 * HA))
            boxed = boxed + jnp.dot(
                edge[s].reshape(STRIPS * 4 * pairs, cols), near, preferred_element_type=F32
            )
        for group in range(STRIPS):
            at = group * 4 * pairs
            re, im, pa, pb = [
                boxed[at + f * pairs : at + (f + 1) * pairs] for f in range(4)
            ]
            value = jnp.sqrt((re * re + im * im) * scale) * lax.rsqrt(pa * pb * scale + 1e-6)
            look = (height // SA) * group + k // SA
            if k % SA == 0:
                coh[look] = value
            else:
                coh[look] += value

    take = ones(
        lax.div(lax.broadcasted_iota(jnp.int32, (cols // SR, 2 * cols), 1) & (cols - 1), SR)
        == lax.broadcasted_iota(jnp.int32, (cols // SR, 2 * cols), 0)
    )

    def mean(value):
        out = lax.dot_general(
            take,
            jnp.concatenate(split(value), axis=1),
            (((1,), (1,)), ((), ())),
            preferred_element_type=F32,
        )
        return out * (1.0 / (SA * SR))

    coh_mean = mean(coh[...].reshape(looks * pairs, cols))
    product_mean = mean(looked[...].reshape(looks * 2 * pairs, cols))
    for g in range(looks):
        coherence_ref[g] = coh_mean[:, g * pairs : (g + 1) * pairs]
        for f in range(2):
            at = (2 * g + f) * pairs
            product_ref[f, g] = product_mean[:, at : at + pairs]


def boxes(lines, core, side, epochs, tiles, halos):
    pairs = epochs.shape[0]
    sides = len(halos) // 2
    rows = tiles[4].shape[0] // HA
    cols = 2 * LANES
    looks = lines // SA
    height = lines // STRIPS
    return pl.pallas_call(
        functools.partial(box_kernel, sides, lines),
        out_shape=[
            jax.ShapeDtypeStruct((looks, cols // SR, pairs), F32),
            jax.ShapeDtypeStruct((2, looks, cols // SR, pairs), F32),
        ],
        in_specs=[smem(), smem()] + [vmem()] * (1 + len(tiles) + len(halos)),
        out_specs=[vmem(), vmem()],
        scratch_shapes=[
            pltpu.VMEM((lines + 2 * HA, 2 * rows, LANES), BF16),
            pltpu.VMEM((lines + 2 * HA, 4 * pairs, cols), F32),
            pltpu.VMEM((height, STRIPS, 4 * pairs, 2 * cols), BF16),
            pltpu.VMEM((sides, STRIPS, 4 * pairs, cols), BF16),
            pltpu.VMEM((looks, pairs, cols), F32),
            pltpu.VMEM((looks, 2 * pairs, cols), F32),
        ],
        compiler_params=params(),
        name="boxes",
    )(core, side, epochs, *[in_vmem(v) for v in (*tiles, *halos)])


def edge_place(start):
    span = LANES // HR
    row = jnp.arange(span * LANES, dtype=jnp.int32)
    column = (row % LANES) - start
    target = jnp.where((column >= 0) & (column < HR), (row // LANES) * HR + column, -1)
    return (target[:, None] == jnp.arange(LANES, dtype=jnp.int32)[None, :]).astype(BF16)


def per_device(volume, band, strip, epochs):
    bursts, height, dates, _, columns = volume.shape
    count, wide = lax.axis_size("az"), lax.axis_size("rg")
    assert columns == 2 * LANES
    lines = STRIPS * height
    rows = dates * 4
    me, rg, core = lax.axis_index("az"), lax.axis_index("rg"), lax.axis_index("dates")
    x = volume.reshape(bursts, height, dates, 2, 2, LANES).transpose(0, 1, 2, 4, 3, 5)
    x = x.reshape(bursts, height * rows, LANES)
    line = count == 4
    ends = (me == 0) | (me == count - 1)
    parts = partial_sums(line, count, me.reshape(1), band.reshape(-1), strip, x)
    if line:
        outer_parts, inner_parts = line_exchange(parts, ends)
        outer = joined_sum(ends, outer_parts)
    else:
        outer = plain_exchange(parts[0])
        inner_parts = [lax.all_to_all(parts[1], "az", split_axis=0, concat_axis=0, tiled=True)]
    step = [(i, i + 1) for i in range(count - 1)]
    top = lax.ppermute(outer[1, (height - HA) * rows :], "az", step)
    bottom = lax.ppermute(outer[0, : HA * rows], "az", [(j, i) for i, j in step])
    swap = [(0, 1), (1, 0)]
    other = lambda v: lax.ppermute(v, "dates", swap)
    if wide == 2:
        side = rg.reshape(1)
        places = [edge_place(jnp.where(rg == 0, LANES - HR, 0))]
        moves = [[(0, 1), (1, 0)]]
    else:
        side = jnp.arange(2, dtype=jnp.int32)
        places = [edge_place(0), edge_place(LANES - HR)]
        up = [(i, i + 1) for i in range(wide - 1)]
        moves = [[(j, i) for i, j in up], up]
    ends = ends.astype(jnp.int32).reshape(1)
    inner, *packed = finish(lines, line, ends, outer, top, bottom, inner_parts, places)
    halos = []
    for value, move in zip(packed, moves):
        halos.append(lax.ppermute(value, "rg", move))
        both = [(2 * i + c, 2 * j + 1 - c) for i, j in move for c in range(2)]
        halos.append(lax.ppermute(value, ("rg", "dates"), both))
    tiles = [
        outer, other(outer), inner, other(inner), top, other(top), bottom, other(bottom),
    ]
    coherence, product = boxes(lines, core.reshape(1), side, epochs, tiles, halos)
    return coherence.transpose(2, 0, 1), product.transpose(3, 0, 1, 2)


def solution(mesh):
    return jax.shard_map(
        per_device,
        mesh=mesh,
        in_specs=(
            P(("groups", "az"), None, "dates", None, "rg"),
            P(("groups", "az"), None),
            P(("groups", "az")),
            P("dates", None),
        ),
        out_specs=(P("dates", ("groups", "az"), "rg"), P("dates", None, ("groups", "az"), "rg")),
        check_vma=False,
    )
```

```python
import functools

import jax
import jax.numpy as jnp
from jax import lax
from jax.experimental import pallas as pl
from jax.experimental.pallas import tpu as pltpu
from jax.sharding import PartitionSpec as P

STRIPS = 4
SA = 4
SR = 16
HA = 2
HR = 10
LANES = 128
F32 = jnp.float32
BF16 = jnp.bfloat16
BUFFER_ROWS = ((0, 3, 1, 2), (1, 0, 2, 3), (2, 3, 1, 0), (3, 0, 2, 1))


def params():
    return pltpu.CompilerParams(vmem_limit_bytes=28 * 1024 * 1024)


def vmem():
    return pl.BlockSpec(memory_space=pltpu.VMEM)


def in_vmem(value):
    return pltpu.with_memory_space_constraint(value, pltpu.VMEM)


def in_hbm(value):
    return pltpu.with_memory_space_constraint(value, pltpu.HBM)


def smem():
    return pl.BlockSpec(memory_space=pltpu.SMEM)


def partial_kernel(line, count, me_ref, band_hbm, strip_hbm, x_hbm, *refs):
    outs, (total, x_ref, band_ref, strip_ref, few, many) = refs[:-6], refs[-6:]
    bursts = x_ref.shape[0]
    tables = [
        pltpu.make_async_copy(band_hbm, band_ref, few.at[0]),
        pltpu.make_async_copy(strip_hbm, strip_ref, few.at[1]),
    ]
    for copy in tables:
        copy.start()
    loads = [pltpu.make_async_copy(x_hbm.at[b], x_ref.at[b], many.at[b]) for b in range(bursts)]
    for copy in loads:
        copy.start()
    total[...] = jnp.zeros_like(total)
    for copy in tables:
        copy.wait()
    for b in range(bursts):
        slot = band_ref[b] * STRIPS + strip_ref[b] + 1
        loads[b].wait()
        total[slot] += x_ref[b].astype(F32)
    height = total.shape[1]
    margin = (outs[0].shape[-2] - STRIPS * height) // 2
    for i in range(count):
        out = outs[i] if line else outs[0].at[i]
        target = jnp.int32(i)
        if line:
            for j, targets in enumerate(BUFFER_ROWS):
                target = jnp.where(me_ref[0] == j, targets[i], target)
        first = target * STRIPS + 1
        out[:margin] = total[first - 1, height - margin :].astype(BF16)
        for strip in range(STRIPS):
            at = margin + strip * height
            out[at : at + height] = total[first + strip].astype(BF16)
        out[margin + STRIPS * height :] = total[first + STRIPS, :margin].astype(BF16)


def partial_sums(line, count, margin, me, band, strip, x):
    bursts, rows = x.shape[:2]
    shape = (STRIPS * rows + 2 * margin, LANES)
    shapes = [shape] * count if line else [(count, *shape)]
    return pl.pallas_call(
        functools.partial(partial_kernel, line, count),
        out_shape=[jax.ShapeDtypeStruct(s, BF16) for s in shapes],
        in_specs=[smem()] + [pl.BlockSpec(memory_space=pl.ANY)] * 3,
        out_specs=[vmem()] * len(shapes),
        scratch_shapes=[
            pltpu.VMEM((count * STRIPS + 2, rows, LANES), F32),
            pltpu.VMEM(x.shape, BF16),
            pltpu.SMEM((bursts,), jnp.int32),
            pltpu.SMEM((bursts,), jnp.int32),
            pltpu.SemaphoreType.DMA((2,)),
            pltpu.SemaphoreType.DMA((bursts,)),
        ],
        compiler_params=params(),
        name="partial_sums",
    )(me, *[in_hbm(v) for v in (band, strip, x)])


def line_exchange(parts, ends):
    own, first, side, far = parts
    near = lax.ppermute(first, "az", [(0, 1), (1, 0), (2, 3), (3, 2)])
    middle = lax.ppermute(side, "az", [(1, 2), (2, 1)])
    joined = jnp.where(ends, far, (far.astype(F32) + near.astype(F32)).astype(BF16))
    joined, side = lax.optimization_barrier((joined, side))
    across = lax.ppermute(joined, "az", [(0, 2), (2, 0), (1, 3), (3, 1)])
    outer = lax.ppermute(side, "az", [(0, 1), (3, 2)])
    return (own, near, middle, across, outer), joined


def finish_kernel(line, ends_ref, *refs):
    parts, refs = refs[: 5 if line else 1], refs[5 if line else 1 :]
    tile, packed = refs[len(refs) // 2], refs[len(refs) // 2 + 1 :]
    places = refs[: len(packed)]
    if line:
        own, near, middle, across, other = [p[...].astype(F32) for p in parts]
        total = own + across + jnp.where(ends_ref[0] == 1, near, middle + other)
    else:
        total = parts[0][0].astype(F32)
        for i in range(1, parts[0].shape[0]):
            total = total + parts[0][i].astype(F32)
    tile[...] = total.astype(BF16)
    groups, rows = packed[0].shape[:2]
    span = places[0].shape[0] // LANES
    height = span - 2 * HA
    spread = jnp.concatenate(
        [
            jnp.concatenate(
                [tile[i * rows : (i + 1) * rows] for i in range(height * g, height * g + span)],
                axis=1,
            )
            for g in range(groups)
        ],
        axis=0,
    )
    for place, out in zip(places, packed):
        got = jnp.dot(spread, place[...], preferred_element_type=F32).astype(BF16)
        out[...] = got.reshape(out.shape)


def finish(line, ends, rows, parts, places):
    operands = [in_vmem(v) for v in (*parts, *places)]
    return pl.pallas_call(
        functools.partial(finish_kernel, line),
        out_shape=[pltpu.VMEM(parts[0].shape[-2:], BF16)]
        + [pltpu.VMEM((STRIPS, rows, LANES), BF16)] * len(places),
        in_specs=[smem()] + [vmem()] * len(operands),
        out_specs=[vmem()] * (1 + len(places)),
        compiler_params=params(),
        name="finish",
    )(ends, *operands)


def ones(condition):
    return jnp.where(condition, 1.0, 0.0).astype(BF16)


def table_kernel(height, core_ref, side_ref, epochs, pick, chosen, near, band, take):
    both = pick.shape[1]
    dates = both // 4
    cols = band.shape[0]
    turned = epochs[...] - (dates // 2) * core_ref[0]
    turned = jnp.where(turned < 0, turned + dates, turned) * 4
    first, second = turned[:, 0:1], turned[:, 1:2]

    def picker(offsets):
        wanted = jnp.concatenate([d + o for d in (first, second) for o in offsets], axis=0)
        return ones(lax.broadcasted_iota(jnp.int32, (wanted.shape[0], both), 1) == wanted)

    pick[...] = picker((0, 1, 2, 3))
    row = lax.broadcasted_iota(jnp.int32, (cols, cols), 0)
    col = lax.broadcasted_iota(jnp.int32, (cols, cols), 1)
    band[...] = ones(jnp.abs(row - col) <= HR)
    row = lax.broadcasted_iota(jnp.int32, (LANES, cols), 0)
    col = lax.broadcasted_iota(jnp.int32, (LANES, cols), 1)
    line_at = lax.div(row, HR)
    column_at = row - line_at * HR
    for s in range(chosen.shape[0]):
        base = side_ref[s] * 2
        chosen[s] = picker((base, base + 1))
        low_side = jnp.where(col <= column_at, 1, 0)
        high_side = jnp.where(col - (cols - HR) >= column_at, 1, 0)
        reach = jnp.where(side_ref[s] == 0, high_side, low_side)
        for k in range(height):
            near[s, k] = ones((reach == 1) & (line_at >= k) & (line_at <= k + 2 * HA))
    row = lax.broadcasted_iota(jnp.int32, take.shape, 0)
    col = lax.broadcasted_iota(jnp.int32, take.shape, 1)
    take[...] = ones(lax.div(row, SR) == (col & (cols // SR - 1)))


def make_tables(height, core, side, epochs, rows):
    pairs = epochs.shape[0]
    sides = side.shape[0]
    cols = 2 * LANES
    shapes = [
        (8 * pairs, 2 * rows),
        (sides, 4 * pairs, 2 * rows),
        (sides, height, LANES, cols),
        (cols, cols),
        (cols, LANES),
    ]
    return pl.pallas_call(
        functools.partial(table_kernel, height),
        out_shape=[pltpu.VMEM(s, BF16) for s in shapes],
        in_specs=[smem(), smem(), vmem()],
        out_specs=[vmem()] * len(shapes),
        compiler_params=params(),
        name="tables",
    )(core, side, epochs)


def fields(ar, ai, br, bi):
    return ar * br + ai * bi, ai * br - ar * bi, ar * ar + ai * ai, br * br + bi * bi


def split(value):
    high = value.astype(BF16)
    return high, (value - high.astype(F32)).astype(BF16)


def pair_kernel(lines, pick, own, other, left, looked, prod):
    rows = pick.shape[1] // 2
    pairs = pick.shape[0] // 8
    height = left.shape[0]
    cols = prod.shape[2]
    for i in range(lines // 2 + HA):
        two = jnp.concatenate(
            [
                jnp.concatenate([v[n * rows : (n + 1) * rows] for v in (own, other)], axis=0)
                for n in (2 * i, 2 * i + 1)
            ],
            axis=1,
        )
        got = jnp.dot(pick[...], two, preferred_element_type=F32)
        part = [got[q * pairs : (q + 1) * pairs] for q in range(8)]
        for ct in range(2):
            parts = fields(part[2 * ct], part[2 * ct + 1], part[4 + 2 * ct], part[5 + 2 * ct])
            for f, value in enumerate(parts):
                at = slice(f * pairs, (f + 1) * pairs)
                lane = slice(ct * LANES, (ct + 1) * LANES)
                prod[2 * i, at, lane] = value[:, :LANES]
                prod[2 * i + 1, at, lane] = value[:, LANES:]
    for g in range(looked.shape[0]):
        for c in range(4 * pairs // 16):
            at = slice(16 * c, 16 * c + 16)
            p = [prod[SA * g + i, at, :] for i in range(SA + 2 * HA)]
            a01, a23, a45, a67 = p[0] + p[1], p[2] + p[3], p[4] + p[5], p[6] + p[7]
            out = (a01 + a23 + p[4], p[1] + a23 + a45, a23 + a45 + p[6], p[3] + a45 + a67)
            for j in range(SA):
                group, k = divmod(SA * g + j, height)
                high, low = split(out[j])
                left[k, group, at, :cols] = high
                left[k, group, at, cols:] = low
            if c < 2 * pairs // 16:
                looked[g, at, :] = a23 + a45


def pair_sums(lines, pick, own, other):
    pairs = pick.shape[0] // 8
    cols = 2 * LANES
    looks = lines // SA
    operands = [in_vmem(v) for v in (pick, own, other)]
    return pl.pallas_call(
        functools.partial(pair_kernel, lines),
        out_shape=[
            pltpu.VMEM((lines // STRIPS, STRIPS, 4 * pairs, 2 * cols), BF16),
            pltpu.VMEM((looks, 2 * pairs, cols), F32),
        ],
        in_specs=[vmem()] * len(operands),
        out_specs=[vmem(), vmem()],
        scratch_shapes=[pltpu.VMEM((lines + 2 * HA, 4 * pairs, cols), F32)],
        compiler_params=params(),
        name="pair_sums",
    )(*operands)


def box_kernel(sides, chosen, near, band, take, left, looked, *refs):
    halos, refs = refs[: 2 * sides], refs[2 * sides :]
    coherence_ref, product_ref, edge, coh = refs
    height, _, fours = left.shape[:3]
    pairs = fours // 4
    cols = band.shape[0]
    looks = looked.shape[0]

    for s in range(sides):
        for group in range(STRIPS):
            value = jnp.concatenate([halos[2 * s][group], halos[2 * s + 1][group]], axis=0)
            got = jnp.dot(chosen[s], value, preferred_element_type=F32)
            part = [got[q * pairs : (q + 1) * pairs] for q in range(4)]
            high, low = split(jnp.concatenate(fields(*part), axis=0))
            edge[s, group, :, :LANES] = high
            edge[s, group, :, LANES:] = low

    scale = 1.0 / float((2 * HA + 1) * (2 * HR + 1)) ** 2
    total = STRIPS * 4 * pairs
    for k in range(height):
        columns = [left[k].reshape(total, 2 * cols)]
        weights = [band[...], band[...]]
        for s in range(sides):
            columns.append(edge[s].reshape(total, cols))
            weights += [near[s, k], near[s, k]]
        boxed = jnp.dot(
            jnp.concatenate(columns, axis=1),
            jnp.concatenate(weights, axis=0),
            preferred_element_type=F32,
        )
        for group in range(STRIPS):
            at = group * 4 * pairs
            re, im, pa, pb = [boxed[at + f * pairs : at + (f + 1) * pairs] for f in range(4)]
            value = jnp.sqrt((re * re + im * im) * scale) * lax.rsqrt(pa * pb * scale + 1e-6)
            look = (height // SA) * group + k // SA
            if k % SA == 0:
                coh[look] = value
            else:
                coh[look] += value

    def mean(value):
        high, low = split(value.reshape(-1, cols))
        out = jnp.dot(
            jnp.concatenate([high, low], axis=1),
            jnp.concatenate([take[...], take[...]], axis=0),
            preferred_element_type=F32,
        )
        return out * (1.0 / (SA * SR))

    each = cols // SR
    coh_mean, product_mean = mean(coh[...]), mean(looked[...])
    mine = lax.div(lax.broadcasted_iota(jnp.int32, (3 * pairs, LANES), 1), each)
    result = jnp.zeros((3 * pairs, LANES), F32)
    for g in range(looks):
        rows_of = jnp.concatenate(
            [
                product_mean[2 * g * pairs : 2 * (g + 1) * pairs],
                coh_mean[g * pairs : (g + 1) * pairs],
            ],
            axis=0,
        )
        result = jnp.where(mine == g, rows_of, result)
    turned = jnp.transpose(result)
    for f, out in enumerate((product_ref.at[0], product_ref.at[1], coherence_ref)):
        out[...] = turned[: looks * each, f * pairs : (f + 1) * pairs].reshape(looks, each, pairs)


def boxes(tables, left, looked, halos):
    looks, pairs = looked.shape[0], looked.shape[1] // 2
    sides = len(halos) // 2
    cols = 2 * LANES
    assert looks * (cols // SR) == LANES
    operands = [in_vmem(v) for v in (*tables, left, looked, *halos)]
    return pl.pallas_call(
        functools.partial(box_kernel, sides),
        out_shape=[
            jax.ShapeDtypeStruct((looks, cols // SR, pairs), F32),
            jax.ShapeDtypeStruct((2, looks, cols // SR, pairs), F32),
        ],
        in_specs=[vmem()] * len(operands),
        out_specs=[vmem(), vmem()],
        scratch_shapes=[
            pltpu.VMEM((sides, STRIPS, 4 * pairs, cols), BF16),
            pltpu.VMEM((looks, pairs, cols), F32),
        ],
        compiler_params=params(),
        name="boxes",
    )(*operands)


def edge_place(span, start):
    row = jnp.arange(span * LANES, dtype=jnp.int32)
    column = (row % LANES) - start
    target = jnp.where((column >= 0) & (column < HR), (row // LANES) * HR + column, -1)
    return (target[:, None] == jnp.arange(LANES, dtype=jnp.int32)[None, :]).astype(BF16)


def per_device(volume, band, strip, epochs):
    bursts, height, dates, _, columns = volume.shape
    count, wide = lax.axis_size("az"), lax.axis_size("rg")
    assert columns == 2 * LANES
    lines = STRIPS * height
    rows = dates * 4
    me, rg, core = lax.axis_index("az"), lax.axis_index("rg"), lax.axis_index("dates")
    x = volume.reshape(bursts, height, dates, 2, 2, LANES).transpose(0, 1, 2, 4, 3, 5)
    x = x.reshape(bursts, height * rows, LANES)
    line = count == 4
    ends = (me == 0) | (me == count - 1)
    parts = partial_sums(line, count, HA * rows, me.reshape(1), band.reshape(-1), strip, x)
    if line:
        parts, last = line_exchange(parts, ends)
    else:
        last = parts[0]
        parts = [lax.all_to_all(last, "az", split_axis=0, concat_axis=0, tiled=True)]
    epochs, rg, core, last = lax.optimization_barrier((epochs, rg, core, last))
    if wide == 2:
        side = rg.reshape(1)
        starts = [jnp.where(rg == 0, LANES - HR, 0)]
        moves = [[(0, 1), (1, 0)]]
    else:
        side = jnp.arange(2, dtype=jnp.int32)
        starts = [0, LANES - HR]
        up = [(i, i + 1) for i in range(wide - 1)]
        moves = [[(j, i) for i, j in up], up]
    places = [edge_place(height + 2 * HA, start) for start in starts]
    pick, *tables = make_tables(height, core.reshape(1), side, epochs, rows)

    flag = ends.astype(jnp.int32).reshape(1)
    own, *packed = finish(line, flag, rows, parts, places)
    halos = []
    for value, move in zip(packed, moves):
        halos.append(lax.ppermute(value, "rg", move))
        both = [(2 * i + c, 2 * j + 1 - c) for i, j in move for c in range(2)]
        halos.append(lax.ppermute(value, ("rg", "dates"), both))
    other = lax.ppermute(own, "dates", [(0, 1), (1, 0)])
    left, looked = pair_sums(lines, pick, own, other)
    coherence, product = boxes(tables, left, looked, halos)
    return coherence.transpose(2, 0, 1), product.transpose(3, 0, 1, 2)


def solution(mesh):
    return jax.shard_map(
        per_device,
        mesh=mesh,
        in_specs=(
            P(("groups", "az"), None, "dates", None, "rg"),
            P(("groups", "az"), None),
            P(("groups", "az")),
            P("dates", None),
        ),
        out_specs=(P("dates", ("groups", "az"), "rg"), P("dates", None, ("groups", "az"), "rg")),
        check_vma=False,
    )
```

```python
import functools

import jax
import jax.numpy as jnp
from jax import lax
from jax.experimental import pallas as pl
from jax.experimental.pallas import tpu as pltpu
from jax.sharding import PartitionSpec as P

STRIPS = 4
SA = 4
SR = 16
HA = 2
HR = 10
LANES = 128
F32 = jnp.float32
BF16 = jnp.bfloat16
BUFFER_ROWS = ((0, 3, 1, 2), (1, 0, 2, 3), (2, 3, 1, 0), (3, 0, 2, 1))


def params():
    return pltpu.CompilerParams(vmem_limit_bytes=28 * 1024 * 1024)


def vmem():
    return pl.BlockSpec(memory_space=pltpu.VMEM)


def in_vmem(value):
    return pltpu.with_memory_space_constraint(value, pltpu.VMEM)


def in_hbm(value):
    return pltpu.with_memory_space_constraint(value, pltpu.HBM)


def smem():
    return pl.BlockSpec(memory_space=pltpu.SMEM)


def partial_kernel(line, count, me_ref, band_hbm, strip_hbm, x_hbm, *refs):
    outs, (total, x_ref, band_ref, strip_ref, few, many) = refs[:-6], refs[-6:]
    bursts = x_ref.shape[0]
    tables = [
        pltpu.make_async_copy(band_hbm, band_ref, few.at[0]),
        pltpu.make_async_copy(strip_hbm, strip_ref, few.at[1]),
    ]
    for copy in tables:
        copy.start()
    loads = [pltpu.make_async_copy(x_hbm.at[b], x_ref.at[b], many.at[b]) for b in range(bursts)]
    for copy in loads:
        copy.start()
    total[...] = jnp.zeros_like(total)
    for copy in tables:
        copy.wait()
    for b in range(bursts):
        slot = band_ref[b] * STRIPS + strip_ref[b] + 1
        loads[b].wait()
        total[slot] += x_ref[b].astype(F32)
    height = total.shape[1]
    margin = (outs[0].shape[-2] - STRIPS * height) // 2
    for i in range(count):
        out = outs[i] if line else outs[0].at[i]
        target = jnp.int32(i)
        if line:
            for j, targets in enumerate(BUFFER_ROWS):
                target = jnp.where(me_ref[0] == j, targets[i], target)
        first = target * STRIPS + 1
        out[:margin] = total[first - 1, height - margin :].astype(BF16)
        for strip in range(STRIPS):
            at = margin + strip * height
            out[at : at + height] = total[first + strip].astype(BF16)
        out[margin + STRIPS * height :] = total[first + STRIPS, :margin].astype(BF16)


def partial_sums(line, count, margin, me, band, strip, x):
    bursts, rows = x.shape[:2]
    shape = (STRIPS * rows + 2 * margin, LANES)
    shapes = [shape] * count if line else [(count, *shape)]
    return pl.pallas_call(
        functools.partial(partial_kernel, line, count),
        out_shape=[jax.ShapeDtypeStruct(s, BF16) for s in shapes],
        in_specs=[smem()] + [pl.BlockSpec(memory_space=pl.ANY)] * 3,
        out_specs=[vmem()] * len(shapes),
        scratch_shapes=[
            pltpu.VMEM((count * STRIPS + 2, rows, LANES), F32),
            pltpu.VMEM(x.shape, BF16),
            pltpu.SMEM((bursts,), jnp.int32),
            pltpu.SMEM((bursts,), jnp.int32),
            pltpu.SemaphoreType.DMA((2,)),
            pltpu.SemaphoreType.DMA((bursts,)),
        ],
        compiler_params=params(),
        name="partial_sums",
    )(me, *[in_hbm(v) for v in (band, strip, x)])


def line_exchange(parts, ends):
    own, first, side, far = parts
    near = lax.ppermute(first, "az", [(0, 1), (1, 0), (2, 3), (3, 2)])
    middle = lax.ppermute(side, "az", [(1, 2), (2, 1)])
    joined = jnp.where(ends, far, (far.astype(F32) + near.astype(F32)).astype(BF16))
    joined, side = lax.optimization_barrier((joined, side))
    across = lax.ppermute(joined, "az", [(0, 2), (2, 0), (1, 3), (3, 1)])
    outer = lax.ppermute(side, "az", [(0, 1), (3, 2)])
    return (own, near, middle, across, outer), joined


def finish_kernel(line, ends_ref, side_ref, *refs):
    parts, refs = refs[: 5 if line else 1], refs[5 if line else 1 :]
    tile, packed = refs[len(refs) // 2], refs[len(refs) // 2 + 1 :]
    places = refs[: len(packed)]
    if line:
        own, near, middle, across, other = [p[...].astype(F32) for p in parts]
        total = own + across + jnp.where(ends_ref[0] == 1, near, middle + other)
    else:
        total = parts[0][0].astype(F32)
        for i in range(1, parts[0].shape[0]):
            total = total + parts[0][i].astype(F32)
    tile[...] = total.astype(BF16)
    groups = STRIPS
    rows = 2 * packed[0].shape[0] // groups
    span = places[0].shape[0] // LANES
    height = span - 2 * HA
    spread = jnp.concatenate(
        [
            jnp.concatenate(
                [tile[i * rows : (i + 1) * rows] for i in range(height * g, height * g + span)],
                axis=1,
            )
            for g in range(groups)
        ],
        axis=0,
    )
    into = lax.broadcasted_iota(jnp.int32, (groups * rows // 2, groups * rows), 0)
    from_row = lax.broadcasted_iota(jnp.int32, (groups * rows // 2, groups * rows), 1)
    into = 2 * into - (into & 1)
    for s, (place, out) in enumerate(zip(places, packed)):
        got = jnp.dot(spread, place[...], preferred_element_type=F32).astype(BF16)
        keep = ones(from_row == into + 2 * side_ref[s])
        out[...] = jnp.dot(keep, got, preferred_element_type=F32).astype(BF16)


def finish(line, ends, tile, rows, parts, places):
    operands = [in_vmem(v) for v in (*parts, *places)]
    return pl.pallas_call(
        functools.partial(finish_kernel, line),
        out_shape=[pltpu.VMEM(parts[0].shape[-2:], BF16)]
        + [pltpu.VMEM((STRIPS * rows // 2, LANES), BF16)] * len(places),
        in_specs=[smem()] * 2 + [vmem()] * len(operands),
        out_specs=[vmem()] * (1 + len(places)),
        compiler_params=params(),
        name="finish",
    )(ends, tile, *operands)


def ones(condition):
    return jnp.where(condition, 1.0, 0.0).astype(BF16)


def table_kernel(height, core_ref, side_ref, epochs, pick, band, take, chosen, near, look):
    both = pick.shape[1]
    dates = both // 4
    cols = band.shape[0]
    pairs = epochs.shape[0]
    turned = epochs[...] - (dates // 2) * core_ref[0]
    turned = jnp.where(turned < 0, turned + dates, turned)
    first, second = turned[:, 0:1], turned[:, 1:2]

    def picker(rows, columns):
        wanted = jnp.concatenate(rows, axis=0)
        return ones(lax.broadcasted_iota(jnp.int32, (wanted.shape[0], columns), 1) == wanted)

    pick[...] = picker([4 * d + o for d in (first, second) for o in range(4)], both)
    row = lax.broadcasted_iota(jnp.int32, (cols, cols), 0)
    col = lax.broadcasted_iota(jnp.int32, (cols, cols), 1)
    band[...] = ones(jnp.abs(row - col) <= HR)
    row = lax.broadcasted_iota(jnp.int32, take.shape, 0)
    col = lax.broadcasted_iota(jnp.int32, take.shape, 1)
    take[...] = ones(lax.div(row, SR) == (col & (cols // SR - 1)))

    def edge_rows(d):
        half = jnp.where(d >= dates // 2, 1, 0)
        return 2 * d + half * (STRIPS - 1) * dates

    chosen[...] = picker(
        [edge_rows(d) + g * dates + o for d in (first, second) for o in range(2) for g in range(STRIPS)],
        STRIPS * both // 2,
    )
    row = lax.broadcasted_iota(jnp.int32, (LANES, LANES), 0)
    col = lax.broadcasted_iota(jnp.int32, (LANES, LANES), 1)
    line_at = lax.div(row, HR)
    column_at = row - line_at * HR
    slot, column = lax.div(col, SR), col & (SR - 1)
    for s in range(near.shape[0]):
        last = side_ref[s] == 0
        k = jnp.where(last, (slot + 1) & (height - 1), slot)
        reach = jnp.where(last, column - column_at, column_at - column + SR - HR) >= SR - HR
        near[s] = ones(reach & (line_at >= k) & (line_at <= k + 2 * HA))
        part = lax.broadcasted_iota(jnp.int32, (8, LANES), 0)
        lane = lax.div(lax.broadcasted_iota(jnp.int32, (8, LANES), 1), SR)
        lane = jnp.where(last, (lane + 1) & (height - 1), lane)
        look[s] = ones(lax.div(lane, SA) == part)


def make_tables(height, core, side, epochs, rows):
    pairs = epochs.shape[0]
    sides = side.shape[0]
    cols = 2 * LANES
    shapes = [
        (8 * pairs, 2 * rows),
        (cols, cols),
        (cols, LANES),
        (4 * STRIPS * pairs, STRIPS * rows),
        (sides, LANES, LANES),
        (sides, 8, LANES),
    ]
    assert height * SR == LANES
    return pl.pallas_call(
        functools.partial(table_kernel, height),
        out_shape=[pltpu.VMEM(s, BF16) for s in shapes],
        in_specs=[smem(), smem(), vmem()],
        out_specs=[vmem()] * len(shapes),
        compiler_params=params(),
        name="tables",
    )(core, side, epochs)


def fields(ar, ai, br, bi):
    return ar * br + ai * bi, ai * br - ar * bi, ar * ar + ai * ai, br * br + bi * bi


def split(value):
    high = value.astype(BF16)
    return high, (value - high.astype(F32)).astype(BF16)


SCALE = 1.0 / float((2 * HA + 1) * (2 * HR + 1)) ** 2


def ratio(re, im, pa, pb):
    return jnp.sqrt((re * re + im * im) * SCALE) * lax.rsqrt(pa * pb * SCALE + 1e-6)


def pair_kernel(lines, side_ref, pick, band, take, own, other, *refs):
    product_ref, coherence_ref, kept, prod, left, looked, coh = refs
    rows = pick.shape[1] // 2
    pairs = pick.shape[0] // 8
    height = left.shape[0]
    cols = prod.shape[2]
    looks = looked.shape[0]
    for i in range(lines // 2 + HA):
        two = jnp.concatenate(
            [
                jnp.concatenate([v[n * rows : (n + 1) * rows] for v in (own, other)], axis=0)
                for n in (2 * i, 2 * i + 1)
            ],
            axis=1,
        )
        got = jnp.dot(pick[...], two, preferred_element_type=F32)
        part = [got[q * pairs : (q + 1) * pairs] for q in range(8)]
        for ct in range(2):
            parts = fields(part[2 * ct], part[2 * ct + 1], part[4 + 2 * ct], part[5 + 2 * ct])
            for f, value in enumerate(parts):
                at = slice(f * pairs, (f + 1) * pairs)
                lane = slice(ct * LANES, (ct + 1) * LANES)
                prod[2 * i, at, lane] = value[:, :LANES]
                prod[2 * i + 1, at, lane] = value[:, LANES:]
    for g in range(looks):
        for c in range(4 * pairs // 16):
            at = slice(16 * c, 16 * c + 16)
            p = [prod[SA * g + i, at, :] for i in range(SA + 2 * HA)]
            a01, a23, a45, a67 = p[0] + p[1], p[2] + p[3], p[4] + p[5], p[6] + p[7]
            out = (a01 + a23 + p[4], p[1] + a23 + a45, a23 + a45 + p[6], p[3] + a45 + a67)
            for j in range(SA):
                group, k = divmod(SA * g + j, height)
                high, low = split(out[j])
                left[k, group, at, :cols] = high
                left[k, group, at, cols:] = low
            if c < 2 * pairs // 16:
                looked[g, at, :] = a23 + a45

    total = STRIPS * 4 * pairs
    slot = lax.div(lax.broadcasted_iota(jnp.int32, (total, LANES), 1), SR)
    edges = [jnp.zeros((total, LANES), F32) for _ in range(kept.shape[0])]
    for k in range(height):
        boxed = jnp.dot(
            left[k].reshape(total, 2 * cols),
            jnp.concatenate([band[...], band[...]], axis=0),
            preferred_element_type=F32,
        )
        for s in range(len(edges)):
            last = side_ref[s] == 0
            tile = jnp.where(last, boxed[:, LANES:], boxed[:, :LANES])
            mine = slot == jnp.where(last, (k - 1) & (height - 1), k)
            edges[s] = jnp.where(mine, pltpu.roll(tile, k * SR, 1) if k else tile, edges[s])
        for group in range(STRIPS):
            at = group * 4 * pairs
            value = ratio(*[boxed[at + f * pairs : at + (f + 1) * pairs] for f in range(4)])
            look = (height // SA) * group + k // SA
            if k % SA == 0:
                coh[look] = value
            else:
                coh[look] += value
    for s, value in enumerate(edges):
        for group in range(STRIPS):
            for f in range(4):
                at = (group * 4 + f) * pairs
                to = (f * STRIPS + group) * pairs
                kept[s, to : to + pairs] = value[at : at + pairs]

    def mean(value):
        high, low = split(value.reshape(-1, cols))
        out = jnp.dot(
            jnp.concatenate([high, low], axis=1),
            jnp.concatenate([take[...], take[...]], axis=0),
            preferred_element_type=F32,
        )
        return out * (1.0 / (SA * SR))

    each = cols // SR
    coh_mean, product_mean = mean(coh[...]), mean(looked[...])
    mine = lax.div(lax.broadcasted_iota(jnp.int32, (3 * pairs, LANES), 1), each)
    result = jnp.zeros((3 * pairs, LANES), F32)
    for g in range(looks):
        rows_of = jnp.concatenate(
            [
                product_mean[2 * g * pairs : 2 * (g + 1) * pairs],
                coh_mean[g * pairs : (g + 1) * pairs],
            ],
            axis=0,
        )
        result = jnp.where(mine == g, rows_of, result)
    turned = jnp.transpose(result)
    for f, out in enumerate((product_ref.at[0], product_ref.at[1], coherence_ref)):
        out[...] = turned[: looks * each, f * pairs : (f + 1) * pairs].reshape(looks, each, pairs)


def pair_looks(lines, side, pick, band, take, own, other):
    pairs = pick.shape[0] // 8
    sides = side.shape[0]
    cols = 2 * LANES
    looks = lines // SA
    assert looks * (cols // SR) == LANES
    operands = [in_vmem(v) for v in (pick, band, take, own, other)]
    return pl.pallas_call(
        functools.partial(pair_kernel, lines),
        out_shape=[
            jax.ShapeDtypeStruct((2, looks, cols // SR, pairs), F32),
            pltpu.VMEM((looks, cols // SR, pairs), F32),
            pltpu.VMEM((sides, STRIPS * 4 * pairs, LANES), F32),
        ],
        in_specs=[smem()] + [vmem()] * len(operands),
        out_specs=[vmem()] * 3,
        scratch_shapes=[
            pltpu.VMEM((lines + 2 * HA, 4 * pairs, cols), F32),
            pltpu.VMEM((lines // STRIPS, STRIPS, 4 * pairs, 2 * cols), BF16),
            pltpu.VMEM((looks, 2 * pairs, cols), F32),
            pltpu.VMEM((looks, pairs, cols), F32),
        ],
        compiler_params=params(),
        name="pair_looks",
    )(side, *operands)


def edge_kernel(side_ref, chosen, near, look, inner, kept, *refs):
    halos, out = refs[:-1], refs[-1]
    looks, each, pairs = out.shape
    out[...] = inner[...]
    for s in range(kept.shape[0]):
        packed = jnp.concatenate([halos[2 * s][...], halos[2 * s + 1][...]], axis=0)
        got = jnp.dot(chosen[...], packed, preferred_element_type=F32)
        step = STRIPS * pairs
        part = [got[q * step : (q + 1) * step] for q in range(4)]
        high, low = split(jnp.concatenate(fields(*part), axis=0))
        boxed = kept[s] + jnp.dot(
            jnp.concatenate([high, low], axis=1),
            jnp.concatenate([near[s], near[s]], axis=0),
            preferred_element_type=F32,
        )
        high, low = split(ratio(*[boxed[f * step : (f + 1) * step] for f in range(4)]))
        mean = lax.dot_general(
            jnp.concatenate([look[s], look[s]], axis=1),
            jnp.concatenate([high, low], axis=1),
            (((1,), (1,)), ((), ())),
            preferred_element_type=F32,
        ) * (1.0 / (SA * SR))
        column = jnp.where(side_ref[s] == 0, each - 1, 0)
        parts = looks // STRIPS
        for g in range(looks):
            at = (g // parts) * pairs
            out[g, pl.ds(column, 1), :] = mean[g % parts : g % parts + 1, at : at + pairs]


def add_edges(side, chosen, near, look, inner, kept, halos):
    operands = [in_vmem(v) for v in (chosen, near, look, inner, kept, *halos)]
    return pl.pallas_call(
        edge_kernel,
        out_shape=jax.ShapeDtypeStruct(inner.shape, F32),
        in_specs=[smem()] + [vmem()] * len(operands),
        out_specs=vmem(),
        compiler_params=params(),
        name="add_edges",
    )(side, *operands)


def edge_place(span, start):
    row = jnp.arange(span * LANES, dtype=jnp.int32)
    column = (row % LANES) - start
    target = jnp.where((column >= 0) & (column < HR), (row // LANES) * HR + column, -1)
    return (target[:, None] == jnp.arange(LANES, dtype=jnp.int32)[None, :]).astype(BF16)


def per_device(volume, band, strip, epochs):
    bursts, height, dates, _, columns = volume.shape
    count, wide = lax.axis_size("az"), lax.axis_size("rg")
    assert columns == 2 * LANES
    lines = STRIPS * height
    rows = dates * 4
    me, rg, core = lax.axis_index("az"), lax.axis_index("rg"), lax.axis_index("dates")
    x = volume.reshape(bursts, height, dates, 2, 2, LANES).transpose(0, 1, 2, 4, 3, 5)
    x = x.reshape(bursts, height * rows, LANES)
    line = count == 4
    ends = (me == 0) | (me == count - 1)
    parts = partial_sums(line, count, HA * rows, me.reshape(1), band.reshape(-1), strip, x)
    if line:
        parts, last = line_exchange(parts, ends)
    else:
        last = parts[0]
        parts = [lax.all_to_all(last, "az", split_axis=0, concat_axis=0, tiled=True)]
    epochs, rg, core, last = lax.optimization_barrier((epochs, rg, core, last))
    if wide == 2:
        side = rg.reshape(1)
        source = 1 - side
        starts = [jnp.where(rg == 0, LANES - HR, 0)]
        moves = [[(0, 1), (1, 0)]]
    else:
        side = source = jnp.arange(2, dtype=jnp.int32)
        starts = [0, LANES - HR]
        up = [(i, i + 1) for i in range(wide - 1)]
        moves = [[(j, i) for i, j in up], up]
    places = [edge_place(height + 2 * HA, start) for start in starts]
    pick, band, take, *tables = make_tables(height, core.reshape(1), side, epochs, rows)

    flag = ends.astype(jnp.int32).reshape(1)
    own, *packed = finish(line, flag, source, rows, parts, places)
    halos = []
    for value, move in zip(packed, moves):
        halos.append(lax.ppermute(value, "rg", move))
        both = [(2 * i + c, 2 * j + 1 - c) for i, j in move for c in range(2)]
        halos.append(lax.ppermute(value, ("rg", "dates"), both))
    other = lax.ppermute(own, "dates", [(0, 1), (1, 0)])
    product, inner, kept = pair_looks(lines, side, pick, band, take, own, other)
    coherence = add_edges(side, *tables, inner, kept, halos)
    return coherence.transpose(2, 0, 1), product.transpose(3, 0, 1, 2)


def solution(mesh):
    return jax.shard_map(
        per_device,
        mesh=mesh,
        in_specs=(
            P(("groups", "az"), None, "dates", None, "rg"),
            P(("groups", "az"), None),
            P(("groups", "az")),
            P("dates", None),
        ),
        out_specs=(P("dates", ("groups", "az"), "rg"), P("dates", None, ("groups", "az"), "rg")),
        check_vma=False,
    )
```

```python
import functools

import jax
import jax.numpy as jnp
from jax import lax
from jax.experimental import pallas as pl
from jax.experimental.pallas import tpu as pltpu
from jax.sharding import PartitionSpec as P

STRIPS = 4
SA = 4
SR = 16
HA = 2
HR = 10
LANES = 128
F32 = jnp.float32
BF16 = jnp.bfloat16
BUFFER_ROWS = ((0, 3, 1, 2), (1, 0, 2, 3), (2, 3, 1, 0), (3, 0, 2, 1))


def params():
    return pltpu.CompilerParams(vmem_limit_bytes=28 * 1024 * 1024)


def vmem():
    return pl.BlockSpec(memory_space=pltpu.VMEM)


def in_vmem(value):
    return pltpu.with_memory_space_constraint(value, pltpu.VMEM)


def in_hbm(value):
    return pltpu.with_memory_space_constraint(value, pltpu.HBM)


def smem():
    return pl.BlockSpec(memory_space=pltpu.SMEM)


def partial_kernel(line, count, band_hbm, strip_hbm, x_hbm, *refs):
    outs, (total, x_ref, band_ref, strip_ref, few, many) = refs[:-6], refs[-6:]
    bursts = x_ref.shape[0]
    tables = [
        pltpu.make_async_copy(band_hbm, band_ref, few.at[0]),
        pltpu.make_async_copy(strip_hbm, strip_ref, few.at[1]),
    ]
    for copy in tables:
        copy.start()
    loads = [pltpu.make_async_copy(x_hbm.at[b], x_ref.at[b], many.at[b]) for b in range(bursts)]
    for copy in loads:
        copy.start()
    total[...] = jnp.zeros_like(total)
    for copy in tables:
        copy.wait()
    for b in range(bursts):
        slot = band_ref[b] * STRIPS + strip_ref[b] + 1
        loads[b].wait()
        total[slot] += x_ref[b].astype(F32)
    height = total.shape[1]
    margin = (outs[0].shape[-2] - STRIPS * height) // 2
    me = lax.axis_index("az")
    for i in range(count):
        out = outs[i] if line else outs[0].at[i]
        target = jnp.int32(i)
        if line:
            for j, targets in enumerate(BUFFER_ROWS):
                target = jnp.where(me == j, targets[i], target)
        first = target * STRIPS + 1
        out[:margin] = total[first - 1, height - margin :].astype(BF16)
        for strip in range(STRIPS):
            at = margin + strip * height
            out[at : at + height] = total[first + strip].astype(BF16)
        out[margin + STRIPS * height :] = total[first + STRIPS, :margin].astype(BF16)


def partial_sums(line, count, margin, band, strip, x):
    bursts, rows = x.shape[:2]
    shape = (STRIPS * rows + 2 * margin, LANES)
    shapes = [shape] * count if line else [(count, *shape)]
    return pl.pallas_call(
        functools.partial(partial_kernel, line, count),
        out_shape=[jax.ShapeDtypeStruct(s, BF16) for s in shapes],
        in_specs=[pl.BlockSpec(memory_space=pl.ANY)] * 3,
        out_specs=[vmem()] * len(shapes),
        scratch_shapes=[
            pltpu.VMEM((count * STRIPS + 2, rows, LANES), F32),
            pltpu.VMEM(x.shape, BF16),
            pltpu.SMEM((bursts,), jnp.int32),
            pltpu.SMEM((bursts,), jnp.int32),
            pltpu.SemaphoreType.DMA((2,)),
            pltpu.SemaphoreType.DMA((bursts,)),
        ],
        compiler_params=params(),
        name="partial_sums",
    )(*[in_hbm(v) for v in (band, strip, x)])


def at_end():
    me = lax.axis_index("az")
    return (me == 0) | (me == lax.axis_size("az") - 1)


def join_kernel(far, near, out):
    @pl.when(at_end())
    def _():
        out[...] = far[...]

    @pl.when(jnp.logical_not(at_end()))
    def _():
        out[...] = (far[...].astype(F32) + near[...].astype(F32)).astype(BF16)


def join(far, near):
    return pl.pallas_call(
        join_kernel,
        out_shape=pltpu.VMEM(far.shape, BF16),
        in_specs=[vmem()] * 2,
        out_specs=vmem(),
        compiler_params=params(),
        name="join",
    )(in_vmem(far), in_vmem(near))


def line_exchange(parts):
    own, first, side, far = parts
    near = lax.ppermute(first, "az", [(0, 1), (1, 0), (2, 3), (3, 2)])
    middle = lax.ppermute(side, "az", [(1, 2), (2, 1)])
    joined, side = lax.optimization_barrier((join(far, near), side))
    across = lax.ppermute(joined, "az", [(0, 2), (2, 0), (1, 3), (3, 1)])
    outer = lax.ppermute(side, "az", [(0, 1), (3, 2)])
    return (own, near, middle, across, outer), joined


def margin_side(s):
    return lax.axis_index("rg") if lax.axis_size("rg") == 2 else jnp.int32(s)


def sent_tile(s):
    return 1 - lax.axis_index("rg") if lax.axis_size("rg") == 2 else jnp.int32(s)


def finish_kernel(line, *refs):
    parts, refs = refs[: 5 if line else 1], refs[5 if line else 1 :]
    (place, keep), (tile, packed) = refs[:2], refs[2:]
    if line:
        own, near, middle, across, other = [p[...].astype(F32) for p in parts]
        total = own + across + jnp.where(at_end(), near, middle + other)
    else:
        total = parts[0][0].astype(F32)
        for i in range(1, parts[0].shape[0]):
            total = total + parts[0][i].astype(F32)
    tile[...] = total.astype(BF16)
    rows = keep.shape[2] // STRIPS
    span = place.shape[1] // LANES
    height = span - 2 * HA
    spread = jnp.concatenate(
        [
            jnp.concatenate(
                [tile[i * rows : (i + 1) * rows] for i in range(height * g, height * g + span)],
                axis=1,
            )
            for g in range(STRIPS)
        ],
        axis=0,
    )
    for s in range(packed.shape[0]):
        got = jnp.dot(spread, place[s], preferred_element_type=F32).astype(BF16)
        packed[s] = jnp.dot(keep[s], got, preferred_element_type=F32).astype(BF16)


def finish(line, parts, place, keep):
    operands = [in_vmem(v) for v in (*parts, place, keep)]
    return pl.pallas_call(
        functools.partial(finish_kernel, line),
        out_shape=[
            pltpu.VMEM(parts[0].shape[-2:], BF16),
            pltpu.VMEM((keep.shape[0], keep.shape[1], LANES), BF16),
        ],
        in_specs=[vmem()] * len(operands),
        out_specs=[vmem()] * 2,
        compiler_params=params(),
        name="finish",
    )(*operands)


def ones(condition):
    return jnp.where(condition, 1.0, 0.0).astype(BF16)


def table_kernel(height, epochs, place, keep, pick, band, take, chosen, near, look):
    for s in range(place.shape[0]):
        row = lax.broadcasted_iota(jnp.int32, place.shape[1:], 0)
        column = (row & (LANES - 1)) - (LANES - HR) * sent_tile(s)
        target = lax.shift_right_logical(row, 7) * HR + column
        target = jnp.where((column >= 0) & (column < HR), target, -1)
        place[s] = ones(target == lax.broadcasted_iota(jnp.int32, place.shape[1:], 1))
        into = lax.broadcasted_iota(jnp.int32, keep.shape[1:], 0)
        from_row = lax.broadcasted_iota(jnp.int32, keep.shape[1:], 1)
        keep[s] = ones(from_row == 2 * into - (into & 1) + 2 * sent_tile(s))
    both = pick.shape[1]
    dates = both // 4
    cols = band.shape[0]
    pairs = epochs.shape[0]
    turned = epochs[...] - (dates // 2) * lax.axis_index("dates")
    turned = jnp.where(turned < 0, turned + dates, turned)
    first, second = turned[:, 0:1], turned[:, 1:2]

    def picker(rows, columns):
        wanted = jnp.concatenate(rows, axis=0)
        return ones(lax.broadcasted_iota(jnp.int32, (wanted.shape[0], columns), 1) == wanted)

    pick[...] = picker([4 * d + o for d in (first, second) for o in range(4)], both)
    row = lax.broadcasted_iota(jnp.int32, (cols, cols), 0)
    col = lax.broadcasted_iota(jnp.int32, (cols, cols), 1)
    band[...] = ones(jnp.abs(row - col) <= HR)
    row = lax.broadcasted_iota(jnp.int32, take.shape, 0)
    col = lax.broadcasted_iota(jnp.int32, take.shape, 1)
    take[...] = ones(lax.div(row, SR) == (col & (cols // SR - 1)))

    def edge_rows(d):
        half = jnp.where(d >= dates // 2, 1, 0)
        return 2 * d + half * (STRIPS - 1) * dates

    chosen[...] = picker(
        [edge_rows(d) + g * dates + o for d in (first, second) for o in range(2) for g in range(STRIPS)],
        STRIPS * both // 2,
    )
    row = lax.broadcasted_iota(jnp.int32, (LANES, LANES), 0)
    col = lax.broadcasted_iota(jnp.int32, (LANES, LANES), 1)
    line_at = lax.div(row, HR)
    column_at = row - line_at * HR
    slot, column = lax.div(col, SR), col & (SR - 1)
    for s in range(near.shape[0]):
        last = margin_side(s) == 0
        k = jnp.where(last, (slot + 1) & (height - 1), slot)
        reach = jnp.where(last, column - column_at, column_at - column + SR - HR) >= SR - HR
        near[s] = ones(reach & (line_at >= k) & (line_at <= k + 2 * HA))
        part = lax.broadcasted_iota(jnp.int32, (8, LANES), 0)
        lane = lax.div(lax.broadcasted_iota(jnp.int32, (8, LANES), 1), SR)
        lane = jnp.where(last, (lane + 1) & (height - 1), lane)
        look[s] = ones(lax.div(lane, SA) == part)


def make_tables(height, sides, epochs, rows):
    pairs = epochs.shape[0]
    cols = 2 * LANES
    shapes = [
        (sides, (height + 2 * HA) * LANES, LANES),
        (sides, STRIPS * rows // 2, STRIPS * rows),
        (8 * pairs, 2 * rows),
        (cols, cols),
        (cols, LANES),
        (4 * STRIPS * pairs, STRIPS * rows),
        (sides, LANES, LANES),
        (sides, 8, LANES),
    ]
    assert height * SR == LANES
    return pl.pallas_call(
        functools.partial(table_kernel, height),
        out_shape=[pltpu.VMEM(s, BF16) for s in shapes],
        in_specs=[vmem()],
        out_specs=[vmem()] * len(shapes),
        compiler_params=params(),
        name="tables",
    )(epochs)


def fields(ar, ai, br, bi):
    return ar * br + ai * bi, ai * br - ar * bi, ar * ar + ai * ai, br * br + bi * bi


def split(value):
    high = value.astype(BF16)
    return high, (value - high.astype(F32)).astype(BF16)


SCALE = 1.0 / float((2 * HA + 1) * (2 * HR + 1)) ** 2


def ratio(re, im, pa, pb):
    return jnp.sqrt((re * re + im * im) * SCALE) * lax.rsqrt(pa * pb * SCALE + 1e-6)


def pair_kernel(lines, pick, band, take, own, other, *refs):
    product_ref, coherence_ref, kept, prod, left, looked, coh = refs
    rows = pick.shape[1] // 2
    pairs = pick.shape[0] // 8
    height = left.shape[0]
    cols = prod.shape[2]
    looks = looked.shape[0]
    for i in range(lines // 2 + HA):
        two = jnp.concatenate(
            [
                jnp.concatenate([v[n * rows : (n + 1) * rows] for v in (own, other)], axis=0)
                for n in (2 * i, 2 * i + 1)
            ],
            axis=1,
        )
        got = jnp.dot(pick[...], two, preferred_element_type=F32)
        part = [got[q * pairs : (q + 1) * pairs] for q in range(8)]
        for ct in range(2):
            parts = fields(part[2 * ct], part[2 * ct + 1], part[4 + 2 * ct], part[5 + 2 * ct])
            for f, value in enumerate(parts):
                at = slice(f * pairs, (f + 1) * pairs)
                lane = slice(ct * LANES, (ct + 1) * LANES)
                prod[2 * i, at, lane] = value[:, :LANES]
                prod[2 * i + 1, at, lane] = value[:, LANES:]
    for g in range(looks):
        for c in range(4 * pairs // 16):
            at = slice(16 * c, 16 * c + 16)
            p = [prod[SA * g + i, at, :] for i in range(SA + 2 * HA)]
            a01, a23, a45, a67 = p[0] + p[1], p[2] + p[3], p[4] + p[5], p[6] + p[7]
            out = (a01 + a23 + p[4], p[1] + a23 + a45, a23 + a45 + p[6], p[3] + a45 + a67)
            for j in range(SA):
                group, k = divmod(SA * g + j, height)
                high, low = split(out[j])
                left[k, group, at, :cols] = high
                left[k, group, at, cols:] = low
            if c < 2 * pairs // 16:
                looked[g, at, :] = a23 + a45

    total = STRIPS * 4 * pairs
    slot = lax.div(lax.broadcasted_iota(jnp.int32, (total, LANES), 1), SR)
    edges = [jnp.zeros((total, LANES), F32) for _ in range(kept.shape[0])]
    for k in range(height):
        boxed = jnp.dot(
            left[k].reshape(total, 2 * cols),
            jnp.concatenate([band[...], band[...]], axis=0),
            preferred_element_type=F32,
        )
        for s in range(len(edges)):
            last = margin_side(s) == 0
            tile = jnp.where(last, boxed[:, LANES:], boxed[:, :LANES])
            mine = slot == jnp.where(last, (k - 1) & (height - 1), k)
            edges[s] = jnp.where(mine, pltpu.roll(tile, k * SR, 1) if k else tile, edges[s])
        for group in range(STRIPS):
            at = group * 4 * pairs
            value = ratio(*[boxed[at + f * pairs : at + (f + 1) * pairs] for f in range(4)])
            look = (height // SA) * group + k // SA
            if k % SA == 0:
                coh[look] = value
            else:
                coh[look] += value
    for s, value in enumerate(edges):
        for group in range(STRIPS):
            for f in range(4):
                at = (group * 4 + f) * pairs
                to = (f * STRIPS + group) * pairs
                kept[s, to : to + pairs] = value[at : at + pairs]

    def mean(value):
        high, low = split(value.reshape(-1, cols))
        out = jnp.dot(
            jnp.concatenate([high, low], axis=1),
            jnp.concatenate([take[...], take[...]], axis=0),
            preferred_element_type=F32,
        )
        return out * (1.0 / (SA * SR))

    each = cols // SR
    coh_mean, product_mean = mean(coh[...]), mean(looked[...])
    mine = lax.div(lax.broadcasted_iota(jnp.int32, (3 * pairs, LANES), 1), each)
    result = jnp.zeros((3 * pairs, LANES), F32)
    for g in range(looks):
        rows_of = jnp.concatenate(
            [
                product_mean[2 * g * pairs : 2 * (g + 1) * pairs],
                coh_mean[g * pairs : (g + 1) * pairs],
            ],
            axis=0,
        )
        result = jnp.where(mine == g, rows_of, result)
    turned = jnp.transpose(result)
    for f, out in enumerate((product_ref.at[0], product_ref.at[1], coherence_ref)):
        out[...] = turned[: looks * each, f * pairs : (f + 1) * pairs].reshape(looks, each, pairs)


def pair_looks(lines, sides, pick, band, take, own, other):
    pairs = pick.shape[0] // 8
    cols = 2 * LANES
    looks = lines // SA
    assert looks * (cols // SR) == LANES
    operands = [in_vmem(v) for v in (pick, band, take, own, other)]
    return pl.pallas_call(
        functools.partial(pair_kernel, lines),
        out_shape=[
            pltpu.VMEM((2, looks, cols // SR, pairs), F32),
            pltpu.VMEM((looks, cols // SR, pairs), F32),
            pltpu.VMEM((sides, STRIPS * 4 * pairs, LANES), F32),
        ],
        in_specs=[vmem()] * len(operands),
        out_specs=[vmem()] * 3,
        scratch_shapes=[
            pltpu.VMEM((lines + 2 * HA, 4 * pairs, cols), F32),
            pltpu.VMEM((lines // STRIPS, STRIPS, 4 * pairs, 2 * cols), BF16),
            pltpu.VMEM((looks, 2 * pairs, cols), F32),
            pltpu.VMEM((looks, pairs, cols), F32),
        ],
        compiler_params=params(),
        name="pair_looks",
    )(*operands)


def edge_kernel(chosen, near, look, product, inner, kept, *refs):
    halos, (out, product_hbm, done) = refs[:-3], refs[-3:]
    copy = pltpu.make_async_copy(product, product_hbm, done)
    copy.start()
    looks, each, pairs = out.shape
    out[...] = inner[...]
    for s in range(kept.shape[0]):
        packed = jnp.concatenate([halos[2 * s][0], halos[2 * s + 1][0]], axis=0)
        got = jnp.dot(chosen[...], packed, preferred_element_type=F32)
        step = STRIPS * pairs
        part = [got[q * step : (q + 1) * step] for q in range(4)]
        high, low = split(jnp.concatenate(fields(*part), axis=0))
        boxed = kept[s] + jnp.dot(
            jnp.concatenate([high, low], axis=1),
            jnp.concatenate([near[s], near[s]], axis=0),
            preferred_element_type=F32,
        )
        high, low = split(ratio(*[boxed[f * step : (f + 1) * step] for f in range(4)]))
        mean = lax.dot_general(
            jnp.concatenate([look[s], look[s]], axis=1),
            jnp.concatenate([high, low], axis=1),
            (((1,), (1,)), ((), ())),
            preferred_element_type=F32,
        ) * (1.0 / (SA * SR))
        column = jnp.where(margin_side(s) == 0, each - 1, 0)
        parts = looks // STRIPS
        for g in range(looks):
            at = (g // parts) * pairs
            out[g, pl.ds(column, 1), :] = mean[g % parts : g % parts + 1, at : at + pairs]
    copy.wait()


def add_edges(chosen, near, look, product, inner, kept, halos):
    operands = [in_vmem(v) for v in (chosen, near, look, product, inner, kept, *halos)]
    return pl.pallas_call(
        edge_kernel,
        out_shape=[
            jax.ShapeDtypeStruct(inner.shape, F32),
            jax.ShapeDtypeStruct(product.shape, F32),
        ],
        in_specs=[vmem()] * len(operands),
        out_specs=[vmem(), pl.BlockSpec(memory_space=pl.ANY)],
        scratch_shapes=[pltpu.SemaphoreType.DMA],
        compiler_params=params(),
        name="add_edges",
    )(*operands)


def per_device(volume, band, strip, epochs):
    bursts, height, dates, _, columns = volume.shape
    count, wide = lax.axis_size("az"), lax.axis_size("rg")
    assert columns == 2 * LANES
    lines = STRIPS * height
    rows = dates * 4
    x = volume.reshape(bursts, height, dates, 2, 2, LANES).transpose(0, 1, 2, 4, 3, 5)
    x = x.reshape(bursts, height * rows, LANES)
    line = count == 4
    parts = partial_sums(line, count, HA * rows, band.reshape(-1), strip, x)
    if line:
        parts, last = line_exchange(parts)
    else:
        last = parts[0]
        parts = [lax.all_to_all(last, "az", split_axis=0, concat_axis=0, tiled=True)]
    epochs, _ = lax.optimization_barrier((epochs, last))
    up = [(i, i + 1) for i in range(wide - 1)]
    down = [(j, i) for i, j in up]
    moves = [up + down] if wide == 2 else [down, up]
    sides = len(moves)
    place, keep, pick, band, take, *tables = make_tables(height, sides, epochs, rows)
    own, packed = finish(line, parts, place, keep)
    halos = []
    for s, move in enumerate(moves):
        value = packed[s : s + 1]
        halos.append(lax.ppermute(value, "rg", move))
        both = [(2 * i + c, 2 * j + 1 - c) for i, j in move for c in range(2)]
        halos.append(lax.ppermute(value, ("rg", "dates"), both))
    other = lax.ppermute(own, "dates", [(0, 1), (1, 0)])
    product, inner, kept = pair_looks(lines, sides, pick, band, take, own, other)
    coherence, product = add_edges(*tables, product, inner, kept, halos)
    return coherence.transpose(2, 0, 1), product.transpose(3, 0, 1, 2)


def solution(mesh):
    return jax.shard_map(
        per_device,
        mesh=mesh,
        in_specs=(
            P(("groups", "az"), None, "dates", None, "rg"),
            P(("groups", "az"), None),
            P(("groups", "az")),
            P("dates", None),
        ),
        out_specs=(P("dates", ("groups", "az"), "rg"), P("dates", None, ("groups", "az"), "rg")),
        check_vma=False,
    )
```

```python
import functools

import jax
import jax.numpy as jnp
from jax import lax
from jax.experimental import pallas as pl
from jax.experimental.pallas import tpu as pltpu
from jax.sharding import PartitionSpec as P

STRIPS = 4
SA = 4
SR = 16
HA = 2
HR = 10
LANES = 128
F32 = jnp.float32
BF16 = jnp.bfloat16
BUFFER_ROWS = ((0, 3, 1, 2), (1, 0, 2, 3), (2, 3, 1, 0), (3, 0, 2, 1))


def params():
    return pltpu.CompilerParams(vmem_limit_bytes=28 * 1024 * 1024)


def vmem():
    return pl.BlockSpec(memory_space=pltpu.VMEM)


def in_vmem(value):
    return pltpu.with_memory_space_constraint(value, pltpu.VMEM)


def in_hbm(value):
    return pltpu.with_memory_space_constraint(value, pltpu.HBM)


def smem():
    return pl.BlockSpec(memory_space=pltpu.SMEM)


def partial_kernel(line, count, band_hbm, strip_hbm, x_hbm, *refs):
    outs, (total, x_ref, band_ref, strip_ref, few, many) = refs[:-6], refs[-6:]
    bursts = x_ref.shape[0]
    tables = [
        pltpu.make_async_copy(band_hbm, band_ref, few.at[0]),
        pltpu.make_async_copy(strip_hbm, strip_ref, few.at[1]),
    ]
    for copy in tables:
        copy.start()
    loads = [pltpu.make_async_copy(x_hbm.at[b], x_ref.at[b], many.at[b]) for b in range(bursts)]
    for copy in loads:
        copy.start()
    total[...] = jnp.zeros_like(total)
    for copy in tables:
        copy.wait()
    for b in range(bursts):
        slot = band_ref[b] * STRIPS + strip_ref[b] + 1
        loads[b].wait()
        total[slot] += x_ref[b].astype(F32)
    height = total.shape[1]
    margin = (outs[0].shape[-2] - STRIPS * height) // 2
    me = lax.axis_index("az")
    for i in range(count):
        out = outs[i] if line else outs[0].at[i]
        target = jnp.int32(i)
        if line:
            for j, targets in enumerate(BUFFER_ROWS):
                target = jnp.where(me == j, targets[i], target)
        first = target * STRIPS + 1
        out[:margin] = total[first - 1, height - margin :].astype(BF16)
        for strip in range(STRIPS):
            at = margin + strip * height
            out[at : at + height] = total[first + strip].astype(BF16)
        out[margin + STRIPS * height :] = total[first + STRIPS, :margin].astype(BF16)


def partial_sums(line, count, margin, band, strip, x):
    bursts, rows = x.shape[:2]
    shape = (STRIPS * rows + 2 * margin, LANES)
    shapes = [shape] * count if line else [(count, *shape)]
    return pl.pallas_call(
        functools.partial(partial_kernel, line, count),
        out_shape=[jax.ShapeDtypeStruct(s, BF16) for s in shapes],
        in_specs=[pl.BlockSpec(memory_space=pl.ANY)] * 3,
        out_specs=[vmem()] * len(shapes),
        scratch_shapes=[
            pltpu.VMEM((count * STRIPS + 2, rows, LANES), F32),
            pltpu.VMEM(x.shape, BF16),
            pltpu.SMEM((bursts,), jnp.int32),
            pltpu.SMEM((bursts,), jnp.int32),
            pltpu.SemaphoreType.DMA((2,)),
            pltpu.SemaphoreType.DMA((bursts,)),
        ],
        compiler_params=params(),
        name="partial_sums",
    )(*[in_hbm(v) for v in (band, strip, x)])


def at_end():
    me = lax.axis_index("az")
    return (me == 0) | (me == lax.axis_size("az") - 1)


def join_kernel(far, near, out):
    @pl.when(at_end())
    def _():
        out[...] = far[...]

    @pl.when(jnp.logical_not(at_end()))
    def _():
        out[...] = (far[...].astype(F32) + near[...].astype(F32)).astype(BF16)


def join(far, near):
    return pl.pallas_call(
        join_kernel,
        out_shape=pltpu.VMEM(far.shape, BF16),
        in_specs=[vmem()] * 2,
        out_specs=vmem(),
        compiler_params=params(),
        name="join",
    )(in_vmem(far), in_vmem(near))


def line_exchange(parts):
    own, first, side, far = parts
    near = lax.ppermute(first, "az", [(0, 1), (1, 0), (2, 3), (3, 2)])
    middle = lax.ppermute(side, "az", [(1, 2), (2, 1)])
    joined, side = lax.optimization_barrier((join(far, near), side))
    across = lax.ppermute(joined, "az", [(0, 2), (2, 0), (1, 3), (3, 1)])
    outer = lax.ppermute(side, "az", [(0, 1), (3, 2)])
    return (own, near, middle, across, outer), joined


def margin_side(s):
    return lax.axis_index("rg") if lax.axis_size("rg") == 2 else jnp.int32(s)


def sent_tile(s):
    return 1 - lax.axis_index("rg") if lax.axis_size("rg") == 2 else jnp.int32(s)


def finish_kernel(line, *refs):
    parts, refs = refs[: 5 if line else 1], refs[5 if line else 1 :]
    (place, keep), (tile, packed) = refs[:2], refs[2:]
    if line:
        own, near, middle, across, other = [p[...].astype(F32) for p in parts]
        total = own + across + jnp.where(at_end(), near, middle + other)
    else:
        total = parts[0][0].astype(F32)
        for i in range(1, parts[0].shape[0]):
            total = total + parts[0][i].astype(F32)
    tile[...] = total.astype(BF16)
    rows = keep.shape[2] // STRIPS
    span = place.shape[1] // LANES
    height = span - 2 * HA
    for s in range(packed.shape[0]):
        lane = lax.broadcasted_iota(jnp.int32, (rows, LANES), 1)
        start = (LANES - HR) * sent_tile(s)
        groups = []
        for g in range(STRIPS):
            value = jnp.zeros((rows, LANES), F32)
            for i in range(span):
                at = (height * g + i) * rows
                moved = pltpu.roll(tile[at : at + rows].astype(F32), (i * HR - start) & (LANES - 1), 1)
                value = jnp.where((lane >= i * HR) & (lane < (i + 1) * HR), moved, value)
            groups.append(value)
        got = jnp.concatenate(groups, axis=0).astype(BF16)
        packed[s] = jnp.dot(keep[s], got, preferred_element_type=F32).astype(BF16)


def finish(line, parts, place, keep):
    operands = [in_vmem(v) for v in (*parts, place, keep)]
    return pl.pallas_call(
        functools.partial(finish_kernel, line),
        out_shape=[
            pltpu.VMEM(parts[0].shape[-2:], BF16),
            pltpu.VMEM((keep.shape[0], keep.shape[1], LANES), BF16),
        ],
        in_specs=[vmem()] * len(operands),
        out_specs=[vmem()] * 2,
        compiler_params=params(),
        name="finish",
    )(*operands)


def ones(condition):
    return jnp.where(condition, 1.0, 0.0).astype(BF16)


def table_kernel(height, epochs, place, keep, pick, band, take, chosen, near, look):
    for s in range(place.shape[0]):
        row = lax.broadcasted_iota(jnp.int32, place.shape[1:], 0)
        column = (row & (LANES - 1)) - (LANES - HR) * sent_tile(s)
        target = lax.shift_right_logical(row, 7) * HR + column
        target = jnp.where((column >= 0) & (column < HR), target, -1)
        place[s] = ones(target == lax.broadcasted_iota(jnp.int32, place.shape[1:], 1))
        into = lax.broadcasted_iota(jnp.int32, keep.shape[1:], 0)
        from_row = lax.broadcasted_iota(jnp.int32, keep.shape[1:], 1)
        keep[s] = ones(from_row == 2 * into - (into & 1) + 2 * sent_tile(s))
    both = pick.shape[1]
    dates = both // 4
    cols = band.shape[0]
    pairs = epochs.shape[0]
    turned = epochs[...] - (dates // 2) * lax.axis_index("dates")
    turned = jnp.where(turned < 0, turned + dates, turned)
    first, second = turned[:, 0:1], turned[:, 1:2]

    def picker(rows, columns):
        wanted = jnp.concatenate(rows, axis=0)
        return ones(lax.broadcasted_iota(jnp.int32, (wanted.shape[0], columns), 1) == wanted)

    pick[...] = picker([4 * d + o for d in (first, second) for o in range(4)], both)
    row = lax.broadcasted_iota(jnp.int32, (cols, cols), 0)
    col = lax.broadcasted_iota(jnp.int32, (cols, cols), 1)
    band[...] = ones(jnp.abs(row - col) <= HR)
    row = lax.broadcasted_iota(jnp.int32, take.shape, 0)
    col = lax.broadcasted_iota(jnp.int32, take.shape, 1)
    take[...] = ones(lax.div(row, SR) == (col & (cols // SR - 1)))

    def edge_rows(d):
        half = jnp.where(d >= dates // 2, 1, 0)
        return 2 * d + half * (STRIPS - 1) * dates

    chosen[...] = picker(
        [edge_rows(d) + g * dates + o for d in (first, second) for o in range(2) for g in range(STRIPS)],
        STRIPS * both // 2,
    )
    row = lax.broadcasted_iota(jnp.int32, (LANES, LANES), 0)
    col = lax.broadcasted_iota(jnp.int32, (LANES, LANES), 1)
    line_at = lax.div(row, HR)
    column_at = row - line_at * HR
    slot, column = lax.div(col, SR), col & (SR - 1)
    for s in range(near.shape[0]):
        last = margin_side(s) == 0
        k = jnp.where(last, (slot + 1) & (height - 1), slot)
        reach = jnp.where(last, column - column_at, column_at - column + SR - HR) >= SR - HR
        near[s] = ones(reach & (line_at >= k) & (line_at <= k + 2 * HA))
        part = lax.broadcasted_iota(jnp.int32, (8, LANES), 0)
        lane = lax.div(lax.broadcasted_iota(jnp.int32, (8, LANES), 1), SR)
        lane = jnp.where(last, (lane + 1) & (height - 1), lane)
        look[s] = ones(lax.div(lane, SA) == part)


def make_tables(height, sides, epochs, rows):
    pairs = epochs.shape[0]
    cols = 2 * LANES
    shapes = [
        (sides, (height + 2 * HA) * LANES, LANES),
        (sides, STRIPS * rows // 2, STRIPS * rows),
        (8 * pairs, 2 * rows),
        (cols, cols),
        (cols, LANES),
        (4 * STRIPS * pairs, STRIPS * rows),
        (sides, LANES, LANES),
        (sides, 8, LANES),
    ]
    assert height * SR == LANES
    return pl.pallas_call(
        functools.partial(table_kernel, height),
        out_shape=[pltpu.VMEM(s, BF16) for s in shapes],
        in_specs=[vmem()],
        out_specs=[vmem()] * len(shapes),
        compiler_params=params(),
        name="tables",
    )(epochs)


def fields(ar, ai, br, bi):
    return ar * br + ai * bi, ai * br - ar * bi, ar * ar + ai * ai, br * br + bi * bi


def split(value):
    high = value.astype(BF16)
    return high, (value - high.astype(F32)).astype(BF16)


EPSILON = 1e-6 * float((2 * HA + 1) * (2 * HR + 1)) ** 2
TINY = 1.1754944e-38


def ratio(re, im, pa, pb):
    size = re * re + im * im
    return size * lax.rsqrt(jnp.maximum(size, TINY)) * lax.rsqrt(pa * pb + EPSILON)


def pair_kernel(lines, pick, band, take, own, other, *refs):
    product_ref, coherence_ref, kept, prod, looked, coh = refs
    rows = pick.shape[1] // 2
    pairs = pick.shape[0] // 8
    height = lines // STRIPS
    cols = prod.shape[2]
    looks = looked.shape[0]
    fours = 4 * pairs

    def products(i):
        two = jnp.concatenate(
            [
                jnp.concatenate([v[n * rows : (n + 1) * rows] for v in (own, other)], axis=0)
                for n in (2 * i, 2 * i + 1)
            ],
            axis=1,
        )
        got = jnp.dot(pick[...], two, preferred_element_type=F32)
        part = [got[q * pairs : (q + 1) * pairs] for q in range(8)]
        for ct in range(2):
            parts = fields(part[2 * ct], part[2 * ct + 1], part[4 + 2 * ct], part[5 + 2 * ct])
            for f, value in enumerate(parts):
                at = slice(f * pairs, (f + 1) * pairs)
                lane = slice(ct * LANES, (ct + 1) * LANES)
                prod[2 * i, at, lane] = value[:, :LANES]
                prod[2 * i + 1, at, lane] = value[:, LANES:]

    def azimuth(g):
        chunks = []
        for c in range(fours // 16):
            at = slice(16 * c, 16 * c + 16)
            p = [prod[SA * g + i, at, :] for i in range(SA + 2 * HA)]
            a01, a23, a45, a67 = p[0] + p[1], p[2] + p[3], p[4] + p[5], p[6] + p[7]
            out = (a01 + a23 + p[4], p[1] + a23 + a45, a23 + a45 + p[6], p[3] + a45 + a67)
            chunks.append([jnp.concatenate(split(v), axis=1) for v in out])
            if c < 2 * pairs // 16:
                looked[g, at, :] = a23 + a45
        return jnp.concatenate([chunk[j] for j in range(SA) for chunk in chunks], axis=0)

    slot = lax.div(lax.broadcasted_iota(jnp.int32, (fours, LANES), 1), SR)
    sides = kept.shape[0]
    edges = [None] * sides

    def ranges(g, left):
        boxed = jnp.dot(
            left, jnp.concatenate([band[...], band[...]], axis=0), preferred_element_type=F32
        )
        total = None
        for j in range(SA):
            group, k = divmod(SA * g + j, height)
            line = boxed[j * fours : (j + 1) * fours]
            value = ratio(*[line[f * pairs : (f + 1) * pairs] for f in range(4)])
            total = value if total is None else total + value
            for s in range(sides):
                last = margin_side(s) == 0
                tile = jnp.where(last, line[:, LANES:], line[:, :LANES])
                tile = pltpu.roll(tile, k * SR, 1) if k else tile
                mine = slot == jnp.where(last, (k - 1) & (height - 1), k)
                edges[s] = jnp.where(mine, tile, edges[s]) if k else tile
                if k == height - 1:
                    for f in range(4):
                        to = (f * STRIPS + group) * pairs
                        kept[s, to : to + pairs] = edges[s][f * pairs : (f + 1) * pairs]
        coh[g] = total

    ready = 0
    left = None
    for g in range(looks + 1):
        if g < looks:
            while 2 * ready < SA * (g + 1) + 2 * HA:
                products(ready)
                ready += 1
            new = azimuth(g)
        if g:
            ranges(g - 1, left)
        left = new

    def mean(value):
        high, low = split(value.reshape(-1, cols))
        out = jnp.dot(
            jnp.concatenate([high, low], axis=1),
            jnp.concatenate([take[...], take[...]], axis=0),
            preferred_element_type=F32,
        )
        return out * (1.0 / (SA * SR))

    each = cols // SR
    coh_mean, product_mean = mean(coh[...]), mean(looked[...])
    mine = lax.div(lax.broadcasted_iota(jnp.int32, (3 * pairs, LANES), 1), each)
    result = jnp.zeros((3 * pairs, LANES), F32)
    for g in range(looks):
        rows_of = jnp.concatenate(
            [
                product_mean[2 * g * pairs : 2 * (g + 1) * pairs],
                coh_mean[g * pairs : (g + 1) * pairs],
            ],
            axis=0,
        )
        result = jnp.where(mine == g, rows_of, result)
    turned = jnp.transpose(result)
    for f, out in enumerate((product_ref.at[0], product_ref.at[1], coherence_ref)):
        out[...] = turned[: looks * each, f * pairs : (f + 1) * pairs].reshape(looks, each, pairs)


def pair_looks(lines, sides, pick, band, take, own, other):
    pairs = pick.shape[0] // 8
    cols = 2 * LANES
    looks = lines // SA
    assert looks * (cols // SR) == LANES
    operands = [in_vmem(v) for v in (pick, band, take, own, other)]
    return pl.pallas_call(
        functools.partial(pair_kernel, lines),
        out_shape=[
            pltpu.VMEM((2, looks, cols // SR, pairs), F32),
            pltpu.VMEM((looks, cols // SR, pairs), F32),
            pltpu.VMEM((sides, STRIPS * 4 * pairs, LANES), F32),
        ],
        in_specs=[vmem()] * len(operands),
        out_specs=[vmem()] * 3,
        scratch_shapes=[
            pltpu.VMEM((lines + 2 * HA, 4 * pairs, cols), F32),
            pltpu.VMEM((looks, 2 * pairs, cols), F32),
            pltpu.VMEM((looks, pairs, cols), F32),
        ],
        compiler_params=params(),
        name="pair_looks",
    )(*operands)


def edge_kernel(chosen, near, look, product, inner, kept, *refs):
    halos, (out, product_hbm, done) = refs[:-3], refs[-3:]
    copy = pltpu.make_async_copy(product, product_hbm, done)
    copy.start()
    looks, each, pairs = out.shape
    out[...] = inner[...]
    for s in range(kept.shape[0]):
        packed = jnp.concatenate([halos[2 * s][0], halos[2 * s + 1][0]], axis=0)
        got = jnp.dot(chosen[...], packed, preferred_element_type=F32)
        step = STRIPS * pairs
        part = [got[q * step : (q + 1) * step] for q in range(4)]
        high, low = split(jnp.concatenate(fields(*part), axis=0))
        boxed = kept[s] + jnp.dot(
            jnp.concatenate([high, low], axis=1),
            jnp.concatenate([near[s], near[s]], axis=0),
            preferred_element_type=F32,
        )
        high, low = split(ratio(*[boxed[f * step : (f + 1) * step] for f in range(4)]))
        mean = lax.dot_general(
            jnp.concatenate([look[s], look[s]], axis=1),
            jnp.concatenate([high, low], axis=1),
            (((1,), (1,)), ((), ())),
            preferred_element_type=F32,
        ) * (1.0 / (SA * SR))
        column = jnp.where(margin_side(s) == 0, each - 1, 0)
        parts = looks // STRIPS
        for g in range(looks):
            at = (g // parts) * pairs
            out[g, pl.ds(column, 1), :] = mean[g % parts : g % parts + 1, at : at + pairs]
    copy.wait()


def add_edges(chosen, near, look, product, inner, kept, halos):
    operands = [in_vmem(v) for v in (chosen, near, look, product, inner, kept, *halos)]
    return pl.pallas_call(
        edge_kernel,
        out_shape=[
            jax.ShapeDtypeStruct(inner.shape, F32),
            jax.ShapeDtypeStruct(product.shape, F32),
        ],
        in_specs=[vmem()] * len(operands),
        out_specs=[vmem(), pl.BlockSpec(memory_space=pl.ANY)],
        scratch_shapes=[pltpu.SemaphoreType.DMA],
        compiler_params=params(),
        name="add_edges",
    )(*operands)


def per_device(volume, band, strip, epochs):
    bursts, height, dates, _, columns = volume.shape
    count, wide = lax.axis_size("az"), lax.axis_size("rg")
    assert columns == 2 * LANES
    lines = STRIPS * height
    rows = dates * 4
    x = volume.reshape(bursts, height, dates, 2, 2, LANES).transpose(0, 1, 2, 4, 3, 5)
    x = x.reshape(bursts, height * rows, LANES)
    line = count == 4
    parts = partial_sums(line, count, HA * rows, band.reshape(-1), strip, x)
    if line:
        parts, last = line_exchange(parts)
    else:
        last = parts[0]
        parts = [lax.all_to_all(last, "az", split_axis=0, concat_axis=0, tiled=True)]
    epochs, _ = lax.optimization_barrier((epochs, last))
    up = [(i, i + 1) for i in range(wide - 1)]
    down = [(j, i) for i, j in up]
    moves = [up + down] if wide == 2 else [down, up]
    sides = len(moves)
    place, keep, pick, band, take, *tables = make_tables(height, sides, epochs, rows)
    own, packed = finish(line, parts, place, keep)
    halos = []
    for s, move in enumerate(moves):
        value = packed[s : s + 1]
        both = [(2 * i + c, 2 * j + 1 - c) for i, j in move for c in range(2)]
        cross = lax.ppermute(value, ("rg", "dates"), both)
        halos += [lax.ppermute(value, "rg", move), cross]
    other = lax.ppermute(own, "dates", [(0, 1), (1, 0)])
    product, inner, kept = pair_looks(lines, sides, pick, band, take, own, other)
    coherence, product = add_edges(*tables, product, inner, kept, halos)
    return coherence.transpose(2, 0, 1), product.transpose(3, 0, 1, 2)


def solution(mesh):
    return jax.shard_map(
        per_device,
        mesh=mesh,
        in_specs=(
            P(("groups", "az"), None, "dates", None, "rg"),
            P(("groups", "az"), None),
            P(("groups", "az")),
            P("dates", None),
        ),
        out_specs=(P("dates", ("groups", "az"), "rg"), P("dates", None, ("groups", "az"), "rg")),
        check_vma=False,
    )
```

```python
import functools

import jax
import jax.numpy as jnp
from jax import lax
from jax.experimental import pallas as pl
from jax.experimental.pallas import tpu as pltpu
from jax.sharding import PartitionSpec as P

STRIPS = 4
SA = 4
SR = 16
HA = 2
HR = 10
LANES = 128
F32 = jnp.float32
BF16 = jnp.bfloat16
BUFFER_ROWS = ((0, 3, 1, 2), (1, 0, 2, 3), (2, 3, 1, 0), (3, 0, 2, 1))


def params():
    return pltpu.CompilerParams(vmem_limit_bytes=28 * 1024 * 1024)


def vmem():
    return pl.BlockSpec(memory_space=pltpu.VMEM)


def in_vmem(value):
    return pltpu.with_memory_space_constraint(value, pltpu.VMEM)


def in_hbm(value):
    return pltpu.with_memory_space_constraint(value, pltpu.HBM)


def smem():
    return pl.BlockSpec(memory_space=pltpu.SMEM)


def partial_kernel(line, count, band_hbm, strip_hbm, x_hbm, *refs):
    outs, (total, x_ref, band_ref, strip_ref, few, many) = refs[:-6], refs[-6:]
    bursts = x_ref.shape[0]
    tables = [
        pltpu.make_async_copy(band_hbm, band_ref, few.at[0]),
        pltpu.make_async_copy(strip_hbm, strip_ref, few.at[1]),
    ]
    for copy in tables:
        copy.start()
    loads = [pltpu.make_async_copy(x_hbm.at[b], x_ref.at[b], many.at[b]) for b in range(bursts)]
    for copy in loads:
        copy.start()
    total[...] = jnp.zeros_like(total)
    for copy in tables:
        copy.wait()
    for b in range(bursts):
        slot = band_ref[b] * STRIPS + strip_ref[b] + 1
        loads[b].wait()
        total[slot] += x_ref[b].astype(F32)
    height = total.shape[1]
    margin = (outs[0].shape[-2] - STRIPS * height) // 2
    me = lax.axis_index("az")
    for i in range(count):
        out = outs[i] if line else outs[0].at[i]
        target = jnp.int32(i)
        if line:
            for j, targets in enumerate(BUFFER_ROWS):
                target = jnp.where(me == j, targets[i], target)
        first = target * STRIPS + 1
        out[:margin] = total[first - 1, height - margin :].astype(BF16)
        for strip in range(STRIPS):
            at = margin + strip * height
            out[at : at + height] = total[first + strip].astype(BF16)
        out[margin + STRIPS * height :] = total[first + STRIPS, :margin].astype(BF16)


def partial_sums(line, count, margin, band, strip, x):
    bursts, rows = x.shape[:2]
    shape = (STRIPS * rows + 2 * margin, LANES)
    shapes = [shape] * count if line else [(count, *shape)]
    return pl.pallas_call(
        functools.partial(partial_kernel, line, count),
        out_shape=[jax.ShapeDtypeStruct(s, BF16) for s in shapes],
        in_specs=[pl.BlockSpec(memory_space=pl.ANY)] * 3,
        out_specs=[vmem()] * len(shapes),
        scratch_shapes=[
            pltpu.VMEM((count * STRIPS + 2, rows, LANES), F32),
            pltpu.VMEM(x.shape, BF16),
            pltpu.SMEM((bursts,), jnp.int32),
            pltpu.SMEM((bursts,), jnp.int32),
            pltpu.SemaphoreType.DMA((2,)),
            pltpu.SemaphoreType.DMA((bursts,)),
        ],
        compiler_params=params(),
        name="partial_sums",
    )(*[in_hbm(v) for v in (band, strip, x)])


def at_end():
    me = lax.axis_index("az")
    return (me == 0) | (me == lax.axis_size("az") - 1)


def join_kernel(far, near, out):
    @pl.when(at_end())
    def _():
        out[...] = far[...]

    @pl.when(jnp.logical_not(at_end()))
    def _():
        out[...] = (far[...].astype(F32) + near[...].astype(F32)).astype(BF16)


def join(far, near):
    return pl.pallas_call(
        join_kernel,
        out_shape=pltpu.VMEM(far.shape, BF16),
        in_specs=[vmem()] * 2,
        out_specs=vmem(),
        compiler_params=params(),
        name="join",
    )(in_vmem(far), in_vmem(near))


def line_exchange(parts):
    own, first, side, far = parts
    near = lax.ppermute(first, "az", [(0, 1), (1, 0), (2, 3), (3, 2)])
    middle = lax.ppermute(side, "az", [(1, 2), (2, 1)])
    joined, side = lax.optimization_barrier((join(far, near), side))
    across = lax.ppermute(joined, "az", [(0, 2), (2, 0), (1, 3), (3, 1)])
    outer = lax.ppermute(side, "az", [(0, 1), (3, 2)])
    return (own, near, middle, across, outer), joined


def margin_side(s):
    return lax.axis_index("rg") if lax.axis_size("rg") == 2 else jnp.int32(s)


def sent_tile(s):
    return 1 - lax.axis_index("rg") if lax.axis_size("rg") == 2 else jnp.int32(s)


def finish_kernel(line, *refs):
    parts, refs = refs[: 5 if line else 1], refs[5 if line else 1 :]
    keep, tile, packed = refs
    rows = keep.shape[2] // STRIPS
    lines = tile.shape[0] // rows
    height = (lines - 2 * HA) // STRIPS
    span = height + 2 * HA
    sides = packed.shape[0]
    lane = lax.broadcasted_iota(jnp.int32, (rows, LANES), 1)
    groups = [[None] * STRIPS for _ in range(sides)]
    for n in range(lines):
        at = slice(n * rows, (n + 1) * rows)
        if line:
            own, near, middle, across, other = [p[at].astype(F32) for p in parts]
            total = own + across + jnp.where(at_end(), near, middle + other)
        else:
            total = parts[0][0, at].astype(F32)
            for i in range(1, parts[0].shape[0]):
                total = total + parts[0][i, at].astype(F32)
        tile[at] = total.astype(BF16)
        for s in range(sides):
            start = (LANES - HR) * sent_tile(s)
            for g in range(STRIPS):
                i = n - height * g
                if 0 <= i < span:
                    moved = pltpu.roll(total, (i * HR - start) & (LANES - 1), 1)
                    if i:
                        moved = jnp.where(lane >= i * HR, moved, groups[s][g])
                    groups[s][g] = moved
    for s in range(sides):
        blank = jnp.zeros((rows, LANES), F32)
        got = [jnp.where(lane < span * HR, value, blank) for value in groups[s]]
        got = jnp.concatenate(got, axis=0).astype(BF16)
        packed[s] = jnp.dot(keep[s], got, preferred_element_type=F32).astype(BF16)


def finish(line, parts, keep):
    operands = [in_vmem(v) for v in (*parts, keep)]
    return pl.pallas_call(
        functools.partial(finish_kernel, line),
        out_shape=[
            pltpu.VMEM(parts[0].shape[-2:], BF16),
            pltpu.VMEM((keep.shape[0], keep.shape[1], LANES), BF16),
        ],
        in_specs=[vmem()] * len(operands),
        out_specs=[vmem()] * 2,
        compiler_params=params(),
        name="finish",
    )(*operands)


def ones(condition):
    return jnp.where(condition, 1.0, 0.0).astype(BF16)


def table_kernel(height, epochs, keep, pick, band, take, chosen, near, look):
    for s in range(keep.shape[0]):
        into = lax.broadcasted_iota(jnp.int32, keep.shape[1:], 0)
        from_row = lax.broadcasted_iota(jnp.int32, keep.shape[1:], 1)
        keep[s] = ones(from_row == 2 * into - (into & 1) + 2 * sent_tile(s))
    both = pick.shape[1]
    dates = both // 4
    cols = band.shape[0]
    pairs = epochs.shape[0]
    turned = epochs[...] - (dates // 2) * lax.axis_index("dates")
    turned = jnp.where(turned < 0, turned + dates, turned)
    first, second = turned[:, 0:1], turned[:, 1:2]

    def picker(rows, columns):
        wanted = jnp.concatenate(rows, axis=0)
        return ones(lax.broadcasted_iota(jnp.int32, (wanted.shape[0], columns), 1) == wanted)

    pick[...] = picker([4 * d + o for d in (first, second) for o in range(4)], both)
    row = lax.broadcasted_iota(jnp.int32, (cols, cols), 0)
    col = lax.broadcasted_iota(jnp.int32, (cols, cols), 1)
    band[...] = ones(jnp.abs(row - col) <= HR)
    row = lax.broadcasted_iota(jnp.int32, take.shape, 0)
    col = lax.broadcasted_iota(jnp.int32, take.shape, 1)
    take[...] = ones(lax.div(row, SR) == (col & (cols // SR - 1)))

    def edge_rows(d):
        half = jnp.where(d >= dates // 2, 1, 0)
        return 2 * d + half * (STRIPS - 1) * dates

    chosen[...] = picker(
        [edge_rows(d) + g * dates + o for d in (first, second) for o in range(2) for g in range(STRIPS)],
        STRIPS * both // 2,
    )
    row = lax.broadcasted_iota(jnp.int32, (LANES, LANES), 0)
    col = lax.broadcasted_iota(jnp.int32, (LANES, LANES), 1)
    line_at = lax.div(row, HR)
    column_at = row - line_at * HR
    slot, column = lax.div(col, SR), col & (SR - 1)
    for s in range(near.shape[0]):
        last = margin_side(s) == 0
        k = jnp.where(last, (slot + 1) & (height - 1), slot)
        reach = jnp.where(last, column - column_at, column_at - column + SR - HR) >= SR - HR
        near[s] = ones(reach & (line_at >= k) & (line_at <= k + 2 * HA))
        part = lax.broadcasted_iota(jnp.int32, (8, LANES), 0)
        lane = lax.div(lax.broadcasted_iota(jnp.int32, (8, LANES), 1), SR)
        lane = jnp.where(last, (lane + 1) & (height - 1), lane)
        look[s] = ones(lax.div(lane, SA) == part)


def make_tables(height, sides, epochs, rows):
    pairs = epochs.shape[0]
    cols = 2 * LANES
    shapes = [
        (sides, STRIPS * rows // 2, STRIPS * rows),
        (8 * pairs, 2 * rows),
        (cols, cols),
        (cols, LANES),
        (4 * STRIPS * pairs, STRIPS * rows),
        (sides, LANES, LANES),
        (sides, 8, LANES),
    ]
    assert height * SR == LANES
    return pl.pallas_call(
        functools.partial(table_kernel, height),
        out_shape=[pltpu.VMEM(s, BF16) for s in shapes],
        in_specs=[vmem()],
        out_specs=[vmem()] * len(shapes),
        compiler_params=params(),
        name="tables",
    )(epochs)


def fields(ar, ai, br, bi):
    return ar * br + ai * bi, ai * br - ar * bi, ar * ar + ai * ai, br * br + bi * bi


def split(value):
    high = value.astype(BF16)
    return high, (value - high.astype(F32)).astype(BF16)


EPSILON = 1e-6 * float((2 * HA + 1) * (2 * HR + 1)) ** 2
TINY = 1.1754944e-38


def ratio(re, im, pa, pb):
    size = re * re + im * im
    return size * lax.rsqrt(jnp.maximum(size, TINY)) * lax.rsqrt(pa * pb + EPSILON)


def pair_kernel(lines, pick, band, take, own, other, *refs):
    product_ref, coherence_ref, kept, prod, looked, coh = refs
    rows = pick.shape[1] // 2
    pairs = pick.shape[0] // 8
    height = lines // STRIPS
    cols = prod.shape[2]
    looks = looked.shape[0]
    fours = 4 * pairs

    def products(i):
        two = jnp.concatenate(
            [
                jnp.concatenate([v[n * rows : (n + 1) * rows] for v in (own, other)], axis=0)
                for n in (2 * i, 2 * i + 1)
            ],
            axis=1,
        )
        got = jnp.dot(pick[...], two, preferred_element_type=F32)
        part = [got[q * pairs : (q + 1) * pairs] for q in range(8)]
        for ct in range(2):
            parts = fields(part[2 * ct], part[2 * ct + 1], part[4 + 2 * ct], part[5 + 2 * ct])
            for f, value in enumerate(parts):
                at = slice(f * pairs, (f + 1) * pairs)
                lane = slice(ct * LANES, (ct + 1) * LANES)
                prod[2 * i, at, lane] = value[:, :LANES]
                prod[2 * i + 1, at, lane] = value[:, LANES:]

    def azimuth(g):
        chunks = []
        for c in range(fours // 16):
            at = slice(16 * c, 16 * c + 16)
            p = [prod[SA * g + i, at, :] for i in range(SA + 2 * HA)]
            a01, a23, a45, a67 = p[0] + p[1], p[2] + p[3], p[4] + p[5], p[6] + p[7]
            out = (a01 + a23 + p[4], p[1] + a23 + a45, a23 + a45 + p[6], p[3] + a45 + a67)
            chunks.append([jnp.concatenate(split(v), axis=1) for v in out])
            if c < 2 * pairs // 16:
                looked[g, at, :] = a23 + a45
        return jnp.concatenate([chunk[j] for j in range(SA) for chunk in chunks], axis=0)

    slot = lax.div(lax.broadcasted_iota(jnp.int32, (fours, LANES), 1), SR)
    sides = kept.shape[0]
    edges = [None] * sides

    def ranges(g, left):
        boxed = jnp.dot(
            left, jnp.concatenate([band[...], band[...]], axis=0), preferred_element_type=F32
        )
        total = None
        for j in range(SA):
            group, k = divmod(SA * g + j, height)
            line = boxed[j * fours : (j + 1) * fours]
            value = ratio(*[line[f * pairs : (f + 1) * pairs] for f in range(4)])
            total = value if total is None else total + value
            for s in range(sides):
                last = margin_side(s) == 0
                tile = jnp.where(last, line[:, LANES:], line[:, :LANES])
                tile = pltpu.roll(tile, k * SR, 1) if k else tile
                mine = slot == jnp.where(last, (k - 1) & (height - 1), k)
                edges[s] = jnp.where(mine, tile, edges[s]) if k else tile
                if k == height - 1:
                    for f in range(4):
                        to = (f * STRIPS + group) * pairs
                        kept[s, to : to + pairs] = edges[s][f * pairs : (f + 1) * pairs]
        coh[g] = total

    ready = 0
    left = None
    for g in range(looks + 1):
        if g < looks:
            while 2 * ready < SA * (g + 1) + 2 * HA:
                products(ready)
                ready += 1
            new = azimuth(g)
        if g:
            ranges(g - 1, left)
        left = new

    def mean(value):
        high, low = split(value.reshape(-1, cols))
        out = jnp.dot(
            jnp.concatenate([high, low], axis=1),
            jnp.concatenate([take[...], take[...]], axis=0),
            preferred_element_type=F32,
        )
        return out * (1.0 / (SA * SR))

    each = cols // SR
    coh_mean, product_mean = mean(coh[...]), mean(looked[...])
    mine = lax.div(lax.broadcasted_iota(jnp.int32, (3 * pairs, LANES), 1), each)
    result = jnp.zeros((3 * pairs, LANES), F32)
    for g in range(looks):
        rows_of = jnp.concatenate(
            [
                product_mean[2 * g * pairs : 2 * (g + 1) * pairs],
                coh_mean[g * pairs : (g + 1) * pairs],
            ],
            axis=0,
        )
        result = jnp.where(mine == g, rows_of, result)
    turned = jnp.transpose(result)
    for f, out in enumerate((product_ref.at[0], product_ref.at[1], coherence_ref)):
        out[...] = turned[: looks * each, f * pairs : (f + 1) * pairs].reshape(looks, each, pairs)


def pair_looks(lines, sides, pick, band, take, own, other):
    pairs = pick.shape[0] // 8
    cols = 2 * LANES
    looks = lines // SA
    assert looks * (cols // SR) == LANES
    operands = [in_vmem(v) for v in (pick, band, take, own, other)]
    return pl.pallas_call(
        functools.partial(pair_kernel, lines),
        out_shape=[
            pltpu.VMEM((2, looks, cols // SR, pairs), F32),
            pltpu.VMEM((looks, cols // SR, pairs), F32),
            pltpu.VMEM((sides, STRIPS * 4 * pairs, LANES), F32),
        ],
        in_specs=[vmem()] * len(operands),
        out_specs=[vmem()] * 3,
        scratch_shapes=[
            pltpu.VMEM((lines + 2 * HA, 4 * pairs, cols), F32),
            pltpu.VMEM((looks, 2 * pairs, cols), F32),
            pltpu.VMEM((looks, pairs, cols), F32),
        ],
        compiler_params=params(),
        name="pair_looks",
    )(*operands)


def edge_kernel(chosen, near, look, product, inner, kept, *refs):
    halos, (out, product_hbm, done) = refs[:-3], refs[-3:]
    copy = pltpu.make_async_copy(product, product_hbm, done)
    copy.start()
    looks, each, pairs = out.shape
    out[...] = inner[...]
    for s in range(kept.shape[0]):
        packed = jnp.concatenate([halos[2 * s][0], halos[2 * s + 1][0]], axis=0)
        got = jnp.dot(chosen[...], packed, preferred_element_type=F32)
        step = STRIPS * pairs
        part = [got[q * step : (q + 1) * step] for q in range(4)]
        high, low = split(jnp.concatenate(fields(*part), axis=0))
        boxed = kept[s] + jnp.dot(
            jnp.concatenate([high, low], axis=1),
            jnp.concatenate([near[s], near[s]], axis=0),
            preferred_element_type=F32,
        )
        high, low = split(ratio(*[boxed[f * step : (f + 1) * step] for f in range(4)]))
        mean = lax.dot_general(
            jnp.concatenate([look[s], look[s]], axis=1),
            jnp.concatenate([high, low], axis=1),
            (((1,), (1,)), ((), ())),
            preferred_element_type=F32,
        ) * (1.0 / (SA * SR))
        column = jnp.where(margin_side(s) == 0, each - 1, 0)
        parts = looks // STRIPS
        for g in range(looks):
            at = (g // parts) * pairs
            out[g, pl.ds(column, 1), :] = mean[g % parts : g % parts + 1, at : at + pairs]
    copy.wait()


def add_edges(chosen, near, look, product, inner, kept, halos):
    operands = [in_vmem(v) for v in (chosen, near, look, product, inner, kept, *halos)]
    return pl.pallas_call(
        edge_kernel,
        out_shape=[
            jax.ShapeDtypeStruct(inner.shape, F32),
            jax.ShapeDtypeStruct(product.shape, F32),
        ],
        in_specs=[vmem()] * len(operands),
        out_specs=[vmem(), pl.BlockSpec(memory_space=pl.ANY)],
        scratch_shapes=[pltpu.SemaphoreType.DMA],
        compiler_params=params(),
        name="add_edges",
    )(*operands)


def per_device(volume, band, strip, epochs):
    bursts, height, dates, _, columns = volume.shape
    count, wide = lax.axis_size("az"), lax.axis_size("rg")
    assert columns == 2 * LANES
    lines = STRIPS * height
    rows = dates * 4
    x = volume.reshape(bursts, height, dates, 2, 2, LANES).transpose(0, 1, 2, 4, 3, 5)
    x = x.reshape(bursts, height * rows, LANES)
    line = count == 4
    parts = partial_sums(line, count, HA * rows, band.reshape(-1), strip, x)
    if line:
        parts, last = line_exchange(parts)
    else:
        last = parts[0]
        parts = [lax.all_to_all(last, "az", split_axis=0, concat_axis=0, tiled=True)]
    epochs, _ = lax.optimization_barrier((epochs, last))
    up = [(i, i + 1) for i in range(wide - 1)]
    down = [(j, i) for i, j in up]
    moves = [up + down] if wide == 2 else [down, up]
    sides = len(moves)
    keep, pick, band, take, *tables = make_tables(height, sides, epochs, rows)
    own, packed = finish(line, parts, keep)
    halos = []
    for s, move in enumerate(moves):
        value = packed[s : s + 1]
        both = [(2 * i + c, 2 * j + 1 - c) for i, j in move for c in range(2)]
        cross = lax.ppermute(value, ("rg", "dates"), both)
        halos += [lax.ppermute(value, "rg", move), cross]
    other = lax.ppermute(own, "dates", [(0, 1), (1, 0)])
    product, inner, kept = pair_looks(lines, sides, pick, band, take, own, other)
    coherence, product = add_edges(*tables, product, inner, kept, halos)
    return coherence.transpose(2, 0, 1), product.transpose(3, 0, 1, 2)


def solution(mesh):
    return jax.shard_map(
        per_device,
        mesh=mesh,
        in_specs=(
            P(("groups", "az"), None, "dates", None, "rg"),
            P(("groups", "az"), None),
            P(("groups", "az")),
            P("dates", None),
        ),
        out_specs=(P("dates", ("groups", "az"), "rg"), P("dates", None, ("groups", "az"), "rg")),
        check_vma=False,
    )
```

```python
import functools

import jax
import jax.numpy as jnp
from jax import lax
from jax.experimental import pallas as pl
from jax.experimental.pallas import tpu as pltpu
from jax.sharding import PartitionSpec as P

STRIPS = 4
SA = 4
SR = 16
HA = 2
HR = 10
LANES = 128
F32 = jnp.float32
BF16 = jnp.bfloat16
BUFFER_ROWS = ((0, 3, 1, 2), (1, 0, 2, 3), (2, 3, 1, 0), (3, 0, 2, 1))


def params():
    return pltpu.CompilerParams(vmem_limit_bytes=28 * 1024 * 1024)


def vmem():
    return pl.BlockSpec(memory_space=pltpu.VMEM)


def in_vmem(value):
    return pltpu.with_memory_space_constraint(value, pltpu.VMEM)


def in_hbm(value):
    return pltpu.with_memory_space_constraint(value, pltpu.HBM)


def smem():
    return pl.BlockSpec(memory_space=pltpu.SMEM)


def partial_kernel(line, count, band_hbm, strip_hbm, x_hbm, *refs):
    outs, (total, x_ref, band_ref, strip_ref, few, many) = refs[:-6], refs[-6:]
    bursts = x_ref.shape[0]
    tables = [
        pltpu.make_async_copy(band_hbm, band_ref, few.at[0]),
        pltpu.make_async_copy(strip_hbm, strip_ref, few.at[1]),
    ]
    for copy in tables:
        copy.start()
    loads = [pltpu.make_async_copy(x_hbm.at[b], x_ref.at[b], many.at[b]) for b in range(bursts)]
    for copy in loads:
        copy.start()
    total[...] = jnp.zeros_like(total)
    for copy in tables:
        copy.wait()
    for b in range(bursts):
        slot = band_ref[b] * STRIPS + strip_ref[b] + 1
        loads[b].wait()
        total[slot] += x_ref[b].astype(F32)
    height = total.shape[1]
    margin = (outs[0].shape[-2] - STRIPS * height) // 2
    me = lax.axis_index("az")
    for i in range(count):
        out = outs[i] if line else outs[0].at[i]
        target = jnp.int32(i)
        if line:
            for j, targets in enumerate(BUFFER_ROWS):
                target = jnp.where(me == j, targets[i], target)
        first = target * STRIPS + 1
        out[:margin] = total[first - 1, height - margin :].astype(BF16)
        for strip in range(STRIPS):
            at = margin + strip * height
            out[at : at + height] = total[first + strip].astype(BF16)
        out[margin + STRIPS * height :] = total[first + STRIPS, :margin].astype(BF16)


def partial_sums(line, count, margin, band, strip, x):
    bursts, rows = x.shape[:2]
    shape = (STRIPS * rows + 2 * margin, LANES)
    shapes = [shape] * count if line else [(count, *shape)]
    return pl.pallas_call(
        functools.partial(partial_kernel, line, count),
        out_shape=[jax.ShapeDtypeStruct(s, BF16) for s in shapes],
        in_specs=[pl.BlockSpec(memory_space=pl.ANY)] * 3,
        out_specs=[vmem()] * len(shapes),
        scratch_shapes=[
            pltpu.VMEM((count * STRIPS + 2, rows, LANES), F32),
            pltpu.VMEM(x.shape, BF16),
            pltpu.SMEM((bursts,), jnp.int32),
            pltpu.SMEM((bursts,), jnp.int32),
            pltpu.SemaphoreType.DMA((2,)),
            pltpu.SemaphoreType.DMA((bursts,)),
        ],
        compiler_params=params(),
        name="partial_sums",
    )(*[in_hbm(v) for v in (band, strip, x)])


def at_end():
    me = lax.axis_index("az")
    return (me == 0) | (me == lax.axis_size("az") - 1)


def join_kernel(far, near, out):
    @pl.when(at_end())
    def _():
        out[...] = far[...]

    @pl.when(jnp.logical_not(at_end()))
    def _():
        out[...] = (far[...].astype(F32) + near[...].astype(F32)).astype(BF16)


def join(far, near):
    return pl.pallas_call(
        join_kernel,
        out_shape=pltpu.VMEM(far.shape, BF16),
        in_specs=[vmem()] * 2,
        out_specs=vmem(),
        compiler_params=params(),
        name="join",
    )(in_vmem(far), in_vmem(near))


def line_exchange(parts):
    own, first, side, far = parts
    near = lax.ppermute(first, "az", [(0, 1), (1, 0), (2, 3), (3, 2)])
    middle = lax.ppermute(side, "az", [(1, 2), (2, 1)])
    joined, side = lax.optimization_barrier((join(far, near), side))
    across = lax.ppermute(joined, "az", [(0, 2), (2, 0), (1, 3), (3, 1)])
    outer = lax.ppermute(side, "az", [(0, 1), (3, 2)])
    return (own, near, middle, across, outer), joined


def margin_side(s):
    return lax.axis_index("rg") if lax.axis_size("rg") == 2 else jnp.int32(s)


def sent_tile(s):
    return 1 - lax.axis_index("rg") if lax.axis_size("rg") == 2 else jnp.int32(s)


def finish_kernel(line, *refs):
    parts, refs = refs[: 5 if line else 1], refs[5 if line else 1 :]
    keep, tile, packed = refs
    rows = keep.shape[2] // STRIPS
    lines = tile.shape[0] // rows
    height = (lines - 2 * HA) // STRIPS
    span = height + 2 * HA
    sides = packed.shape[0]
    lane = lax.broadcasted_iota(jnp.int32, (rows, LANES), 1)
    def run(sum_of):
        groups = [[None] * STRIPS for _ in range(sides)]
        for n in range(lines):
            at = slice(n * rows, (n + 1) * rows)
            total = sum_of(at)
            tile[at] = total.astype(BF16)
            for s in range(sides):
                start = (LANES - HR) * sent_tile(s)
                for g in range(STRIPS):
                    i = n - height * g
                    if 0 <= i < span:
                        moved = pltpu.roll(total, (i * HR - start) & (LANES - 1), 1)
                        if i:
                            moved = jnp.where(lane >= i * HR, moved, groups[s][g])
                        groups[s][g] = moved
        for s in range(sides):
            blank = jnp.zeros((rows, LANES), F32)
            got = [jnp.where(lane < span * HR, value, blank) for value in groups[s]]
            got = jnp.concatenate(got, axis=0).astype(BF16)
            packed[s] = jnp.dot(keep[s], got, preferred_element_type=F32).astype(BF16)

    if line:
        own, near, middle, across, other = parts

        @pl.when(at_end())
        def _():
            run(lambda at: own[at].astype(F32) + across[at].astype(F32) + near[at].astype(F32))

        @pl.when(jnp.logical_not(at_end()))
        def _():
            run(
                lambda at: (own[at].astype(F32) + across[at].astype(F32))
                + (middle[at].astype(F32) + other[at].astype(F32))
            )
    else:
        run(lambda at: sum(parts[0][i, at].astype(F32) for i in range(parts[0].shape[0])))


def finish(line, parts, keep):
    operands = [in_vmem(v) for v in (*parts, keep)]
    return pl.pallas_call(
        functools.partial(finish_kernel, line),
        out_shape=[
            pltpu.VMEM(parts[0].shape[-2:], BF16),
            pltpu.VMEM((keep.shape[0], keep.shape[1], LANES), BF16),
        ],
        in_specs=[vmem()] * len(operands),
        out_specs=[vmem()] * 2,
        compiler_params=params(),
        name="finish",
    )(*operands)


def ones(condition):
    return jnp.where(condition, 1.0, 0.0).astype(BF16)


def table_kernel(height, epochs, keep, pick, band, take, chosen, near, look):
    for s in range(keep.shape[0]):
        into = lax.broadcasted_iota(jnp.int32, keep.shape[1:], 0)
        from_row = lax.broadcasted_iota(jnp.int32, keep.shape[1:], 1)
        keep[s] = ones(from_row == 2 * into - (into & 1) + 2 * sent_tile(s))
    both = pick.shape[1]
    dates = both // 4
    cols = band.shape[0]
    pairs = epochs.shape[0]
    turned = epochs[...] - (dates // 2) * lax.axis_index("dates")
    turned = jnp.where(turned < 0, turned + dates, turned)
    first, second = turned[:, 0:1], turned[:, 1:2]

    def picker(rows, columns):
        wanted = jnp.concatenate(rows, axis=0)
        return ones(lax.broadcasted_iota(jnp.int32, (wanted.shape[0], columns), 1) == wanted)

    pick[...] = picker([4 * d + o for d in (first, second) for o in range(4)], both)
    row = lax.broadcasted_iota(jnp.int32, (cols, cols), 0)
    col = lax.broadcasted_iota(jnp.int32, (cols, cols), 1)
    band[...] = ones(jnp.abs(row - col) <= HR)
    row = lax.broadcasted_iota(jnp.int32, take.shape, 0)
    col = lax.broadcasted_iota(jnp.int32, take.shape, 1)
    take[...] = ones(lax.div(row, SR) == (col & (cols // SR - 1)))

    def edge_rows(d):
        half = jnp.where(d >= dates // 2, 1, 0)
        return 2 * d + half * (STRIPS - 1) * dates

    chosen[...] = picker(
        [edge_rows(d) + g * dates + o for d in (first, second) for o in range(2) for g in range(STRIPS)],
        STRIPS * both // 2,
    )
    row = lax.broadcasted_iota(jnp.int32, (LANES, LANES), 0)
    col = lax.broadcasted_iota(jnp.int32, (LANES, LANES), 1)
    line_at = lax.div(row, HR)
    column_at = row - line_at * HR
    slot, column = lax.div(col, SR), col & (SR - 1)
    for s in range(near.shape[0]):
        last = margin_side(s) == 0
        k = jnp.where(last, (slot + 1) & (height - 1), slot)
        reach = jnp.where(last, column - column_at, column_at - column + SR - HR) >= SR - HR
        near[s] = ones(reach & (line_at >= k) & (line_at <= k + 2 * HA))
        part = lax.broadcasted_iota(jnp.int32, (8, LANES), 0)
        lane = lax.div(lax.broadcasted_iota(jnp.int32, (8, LANES), 1), SR)
        lane = jnp.where(last, (lane + 1) & (height - 1), lane)
        look[s] = ones(lax.div(lane, SA) == part)


def make_tables(height, sides, epochs, rows):
    pairs = epochs.shape[0]
    cols = 2 * LANES
    shapes = [
        (sides, STRIPS * rows // 2, STRIPS * rows),
        (8 * pairs, 2 * rows),
        (cols, cols),
        (cols, LANES),
        (4 * STRIPS * pairs, STRIPS * rows),
        (sides, LANES, LANES),
        (sides, 8, LANES),
    ]
    assert height * SR == LANES
    return pl.pallas_call(
        functools.partial(table_kernel, height),
        out_shape=[pltpu.VMEM(s, BF16) for s in shapes],
        in_specs=[vmem()],
        out_specs=[vmem()] * len(shapes),
        compiler_params=params(),
        name="tables",
    )(epochs)


def fields(ar, ai, br, bi):
    return ar * br + ai * bi, ai * br - ar * bi, ar * ar + ai * ai, br * br + bi * bi


def split(value):
    high = value.astype(BF16)
    return high, (value - high.astype(F32)).astype(BF16)


EPSILON = 1e-6 * float((2 * HA + 1) * (2 * HR + 1)) ** 2
TINY = 1.1754944e-38


def ratio(re, im, pa, pb):
    size = re * re + im * im
    return size * lax.rsqrt(jnp.maximum(size, TINY)) * lax.rsqrt(pa * pb + EPSILON)


def pair_kernel(lines, pick, band, take, own, other, *refs):
    product_ref, coherence_ref, kept, prod, looked, coh = refs
    rows = pick.shape[1] // 2
    pairs = pick.shape[0] // 8
    height = lines // STRIPS
    cols = prod.shape[2]
    looks = looked.shape[0]
    fours = 4 * pairs

    def products(i):
        two = jnp.concatenate(
            [
                jnp.concatenate([v[n * rows : (n + 1) * rows] for v in (own, other)], axis=0)
                for n in (2 * i, 2 * i + 1)
            ],
            axis=1,
        )
        got = jnp.dot(pick[...], two, preferred_element_type=F32)
        part = [got[q * pairs : (q + 1) * pairs] for q in range(8)]
        for ct in range(2):
            parts = fields(part[2 * ct], part[2 * ct + 1], part[4 + 2 * ct], part[5 + 2 * ct])
            for f, value in enumerate(parts):
                at = slice(f * pairs, (f + 1) * pairs)
                lane = slice(ct * LANES, (ct + 1) * LANES)
                prod[2 * i, at, lane] = value[:, :LANES]
                prod[2 * i + 1, at, lane] = value[:, LANES:]

    def azimuth(g):
        chunks = []
        for c in range(fours // 16):
            at = slice(16 * c, 16 * c + 16)
            p = [prod[SA * g + i, at, :] for i in range(SA + 2 * HA)]
            a01, a23, a45, a67 = p[0] + p[1], p[2] + p[3], p[4] + p[5], p[6] + p[7]
            out = (a01 + a23 + p[4], p[1] + a23 + a45, a23 + a45 + p[6], p[3] + a45 + a67)
            chunks.append([jnp.concatenate(split(v), axis=1) for v in out])
            if c < 2 * pairs // 16:
                looked[g, at, :] = a23 + a45
        return jnp.concatenate([chunk[j] for j in range(SA) for chunk in chunks], axis=0)

    slot = lax.div(lax.broadcasted_iota(jnp.int32, (fours, LANES), 1), SR)
    sides = kept.shape[0]
    edges = [None] * sides

    def ranges(g, left):
        boxed = jnp.dot(
            left, jnp.concatenate([band[...], band[...]], axis=0), preferred_element_type=F32
        )
        total = None
        for j in range(SA):
            group, k = divmod(SA * g + j, height)
            line = boxed[j * fours : (j + 1) * fours]
            value = ratio(*[line[f * pairs : (f + 1) * pairs] for f in range(4)])
            total = value if total is None else total + value
            for s in range(sides):
                last = margin_side(s) == 0
                tile = jnp.where(last, line[:, LANES:], line[:, :LANES])
                tile = pltpu.roll(tile, k * SR, 1) if k else tile
                mine = slot == jnp.where(last, (k - 1) & (height - 1), k)
                edges[s] = jnp.where(mine, tile, edges[s]) if k else tile
                if k == height - 1:
                    for f in range(4):
                        to = (f * STRIPS + group) * pairs
                        kept[s, to : to + pairs] = edges[s][f * pairs : (f + 1) * pairs]
        coh[g] = total

    ready = 0
    left = None
    for g in range(looks + 1):
        if g < looks:
            while 2 * ready < SA * (g + 1) + 2 * HA:
                products(ready)
                ready += 1
            new = azimuth(g)
        if g:
            ranges(g - 1, left)
        left = new

    def mean(value):
        high, low = split(value.reshape(-1, cols))
        out = jnp.dot(
            jnp.concatenate([high, low], axis=1),
            jnp.concatenate([take[...], take[...]], axis=0),
            preferred_element_type=F32,
        )
        return out * (1.0 / (SA * SR))

    each = cols // SR
    coh_mean, product_mean = mean(coh[...]), mean(looked[...])
    mine = lax.div(lax.broadcasted_iota(jnp.int32, (3 * pairs, LANES), 1), each)
    result = jnp.zeros((3 * pairs, LANES), F32)
    for g in range(looks):
        rows_of = jnp.concatenate(
            [
                product_mean[2 * g * pairs : 2 * (g + 1) * pairs],
                coh_mean[g * pairs : (g + 1) * pairs],
            ],
            axis=0,
        )
        result = jnp.where(mine == g, rows_of, result)
    turned = jnp.transpose(result)
    for f, out in enumerate((product_ref.at[0], product_ref.at[1], coherence_ref)):
        out[...] = turned[: looks * each, f * pairs : (f + 1) * pairs].reshape(looks, each, pairs)


def pair_looks(lines, sides, pick, band, take, own, other):
    pairs = pick.shape[0] // 8
    cols = 2 * LANES
    looks = lines // SA
    assert looks * (cols // SR) == LANES
    operands = [in_vmem(v) for v in (pick, band, take, own, other)]
    return pl.pallas_call(
        functools.partial(pair_kernel, lines),
        out_shape=[
            pltpu.VMEM((2, looks, cols // SR, pairs), F32),
            pltpu.VMEM((looks, cols // SR, pairs), F32),
            pltpu.VMEM((sides, STRIPS * 4 * pairs, LANES), F32),
        ],
        in_specs=[vmem()] * len(operands),
        out_specs=[vmem()] * 3,
        scratch_shapes=[
            pltpu.VMEM((lines + 2 * HA, 4 * pairs, cols), F32),
            pltpu.VMEM((looks, 2 * pairs, cols), F32),
            pltpu.VMEM((looks, pairs, cols), F32),
        ],
        compiler_params=params(),
        name="pair_looks",
    )(*operands)


def edge_kernel(chosen, near, look, product, inner, kept, *refs):
    halos, (out, product_hbm, done) = refs[:-3], refs[-3:]
    copy = pltpu.make_async_copy(product, product_hbm, done)
    copy.start()
    looks, each, pairs = out.shape
    out[...] = inner[...]
    for s in range(kept.shape[0]):
        packed = jnp.concatenate([halos[2 * s][0], halos[2 * s + 1][0]], axis=0)
        got = jnp.dot(chosen[...], packed, preferred_element_type=F32)
        step = STRIPS * pairs
        part = [got[q * step : (q + 1) * step] for q in range(4)]
        high, low = split(jnp.concatenate(fields(*part), axis=0))
        boxed = kept[s] + jnp.dot(
            jnp.concatenate([high, low], axis=1),
            jnp.concatenate([near[s], near[s]], axis=0),
            preferred_element_type=F32,
        )
        high, low = split(ratio(*[boxed[f * step : (f + 1) * step] for f in range(4)]))
        mean = lax.dot_general(
            jnp.concatenate([look[s], look[s]], axis=1),
            jnp.concatenate([high, low], axis=1),
            (((1,), (1,)), ((), ())),
            preferred_element_type=F32,
        ) * (1.0 / (SA * SR))
        column = jnp.where(margin_side(s) == 0, each - 1, 0)
        parts = looks // STRIPS
        for g in range(looks):
            at = (g // parts) * pairs
            out[g, pl.ds(column, 1), :] = mean[g % parts : g % parts + 1, at : at + pairs]
    copy.wait()


def add_edges(chosen, near, look, product, inner, kept, halos):
    operands = [in_vmem(v) for v in (chosen, near, look, product, inner, kept, *halos)]
    return pl.pallas_call(
        edge_kernel,
        out_shape=[
            jax.ShapeDtypeStruct(inner.shape, F32),
            jax.ShapeDtypeStruct(product.shape, F32),
        ],
        in_specs=[vmem()] * len(operands),
        out_specs=[vmem(), pl.BlockSpec(memory_space=pl.ANY)],
        scratch_shapes=[pltpu.SemaphoreType.DMA],
        compiler_params=params(),
        name="add_edges",
    )(*operands)


def per_device(volume, band, strip, epochs):
    bursts, height, dates, _, columns = volume.shape
    count, wide = lax.axis_size("az"), lax.axis_size("rg")
    assert columns == 2 * LANES
    lines = STRIPS * height
    rows = dates * 4
    x = volume.reshape(bursts, height, dates, 2, 2, LANES).transpose(0, 1, 2, 4, 3, 5)
    x = x.reshape(bursts, height * rows, LANES)
    line = count == 4
    parts = partial_sums(line, count, HA * rows, band.reshape(-1), strip, x)
    if line:
        parts, last = line_exchange(parts)
    else:
        last = parts[0]
        parts = [lax.all_to_all(last, "az", split_axis=0, concat_axis=0, tiled=True)]
    epochs, _ = lax.optimization_barrier((epochs, last))
    up = [(i, i + 1) for i in range(wide - 1)]
    down = [(j, i) for i, j in up]
    moves = [up + down] if wide == 2 else [down, up]
    sides = len(moves)
    keep, pick, band, take, *tables = make_tables(height, sides, epochs, rows)
    own, packed = finish(line, parts, keep)
    halos = []
    for s, move in enumerate(moves):
        value = packed[s : s + 1]
        both = [(2 * i + c, 2 * j + 1 - c) for i, j in move for c in range(2)]
        cross = lax.ppermute(value, ("rg", "dates"), both)
        halos += [lax.ppermute(value, "rg", move), cross]
    other = lax.ppermute(own, "dates", [(0, 1), (1, 0)])
    product, inner, kept = pair_looks(lines, sides, pick, band, take, own, other)
    coherence, product = add_edges(*tables, product, inner, kept, halos)
    return coherence.transpose(2, 0, 1), product.transpose(3, 0, 1, 2)


def solution(mesh):
    return jax.shard_map(
        per_device,
        mesh=mesh,
        in_specs=(
            P(("groups", "az"), None, "dates", None, "rg"),
            P(("groups", "az"), None),
            P(("groups", "az")),
            P("dates", None),
        ),
        out_specs=(P("dates", ("groups", "az"), "rg"), P("dates", None, ("groups", "az"), "rg")),
        check_vma=False,
    )
```
